256 devices in a mesh: seq: 64 (over z, y, core), tensor: 4 (over x).
Axes of the slice: x: 4, y: 4, z: 8, core: 2. Of those that a mesh axis runs over, the one named last changes fastest.
Arguments:
- queries: bfloat16 [8192, 4096], P('seq', 'tensor'), may hold values from -6 to 6
- rollout_suffix_keys: bfloat16 [8192, 512], P('seq', 'tensor'), may hold values from -6 to 6
- rollout_suffix_values: bfloat16 [8192, 512], P('seq', 'tensor'), may hold values from -6 to 6
- blockwise_prefix_keys: bfloat16 [8192, 512], P('seq', 'tensor'), may hold values from -6 to 6
- blockwise_prefix_values: bfloat16 [8192, 512], P('seq', 'tensor'), may hold values from -6 to 6
- block_prompt: int32 [64], P('seq'), may hold values from 0 to 7, as said below
- rollout_prompt: int32 [64], P('seq'), may hold values from 0 to 7, as said below
- suffix_length: int32 [64], P('seq'), may hold values from 32 to 128, as said below
- out_weight: bfloat16 [4096, 2560], P('tensor'), may hold values from -0.09375 to 0.09375
- out_grad: bfloat16 [8192, 2560], P('seq', 'tensor'), may hold values from -6 to 6
Outputs:
- projected: bfloat16 [8192, 2560], P('seq', 'tensor')
- d_queries: bfloat16 [8192, 4096], P('seq', 'tensor')
- d_suffix_keys: bfloat16 [8192, 512], P('seq', 'tensor')
- d_suffix_values: bfloat16 [8192, 512], P('seq', 'tensor')
- d_prefix_keys: bfloat16 [8192, 512], P('seq', 'tensor')
- d_prefix_values: bfloat16 [8192, 512], P('seq', 'tensor')
The draws below stay inside these ranges and needn't reach their ends.
Inputs may be any that keep to these rules, and one draw needn't show every extreme that they name: `block_prompt`: each prompt owns exactly 8 blocks. `rollout_prompt`: each prompt has exactly 8 rollouts. `suffix_length`: some rollout has length 128.
All inputs are finite; a program needn't handle non-finite values.
Results may differ from the reference program's by a relative error of at most 0.039.
Values may be sent and summed in bfloat16 or wider, within the bound.
No kernel may reach another device: no remote copies, remote signals or barrier semaphores. Data moves between devices by JAX's collectives and lax.ppermute only.
A program may use at most 64 MiB of HBM per device.

```python
import jax
import jax.numpy as jnp
from jax import lax

D = 2560
LOCAL_Q_HEADS = 32
LOCAL_KV_HEADS = 4
HEAD_WIDTH = 128
BLOCK_TOKENS = 128
PROMPTS = 8
SUFFIX_SLOTS = 128
GROUP_QUERIES = 8
ROLLOUT_COUNT = 64
SUFFIX_TOTAL = 8192
PREFIX_BLOCKS = 64
PREFIX_TOKENS = 8192


def draw_queries(key, part):
    key = jax.random.fold_in(key, 11)
    array_layout = (ROLLOUT_COUNT, SUFFIX_SLOTS, LOCAL_KV_HEADS, GROUP_QUERIES, HEAD_WIDTH)
    value_entries = jnp.clip(jax.random.normal(key, array_layout, jnp.float32), -6.0, 6.0)
    return value_entries.reshape(SUFFIX_TOTAL, LOCAL_Q_HEADS * HEAD_WIDTH).astype(jnp.bfloat16)


def draw_rollout_suffix_keys(key, part):
    key = jax.random.fold_in(key, 13)
    array_layout = (ROLLOUT_COUNT, SUFFIX_SLOTS, LOCAL_KV_HEADS, HEAD_WIDTH)
    value_entries = jnp.clip(jax.random.normal(key, array_layout, jnp.float32), -6.0, 6.0)
    return value_entries.reshape(SUFFIX_TOTAL, LOCAL_KV_HEADS * HEAD_WIDTH).astype(jnp.bfloat16)


def draw_suffix_length(key, part):
    key = jax.random.fold_in(key, 17)
    first, second = jax.random.split(key)
    lengths = jax.random.randint(first, (ROLLOUT_COUNT,), SUFFIX_SLOTS // 4, SUFFIX_SLOTS + 1)
    picked = jax.random.randint(second, (), 0, ROLLOUT_COUNT)
    return jnp.where(jnp.arange(ROLLOUT_COUNT) == picked, SUFFIX_SLOTS, lengths).astype(jnp.int32)


def draw_rollout_prompt(key, part):
    key = jax.random.fold_in(key, 19)
    shuffled = jax.random.permutation(key, ROLLOUT_COUNT)
    return (shuffled // (ROLLOUT_COUNT // PROMPTS)).astype(jnp.int32)


def draw_block_prompt(key, part):
    key = jax.random.fold_in(key, 23)
    shuffled = jax.random.permutation(key, PREFIX_BLOCKS)
    return (shuffled // (PREFIX_BLOCKS // PROMPTS)).astype(jnp.int32)


def levels(own_key, dims, shards, least, largest):
    level, own = 1.0, jax.random.fold_in(own_key, 6)
    for axis_at, blocks in shards:
        steps = jnp.exp(jax.random.uniform(jax.random.fold_in(own, axis_at), (blocks,), jnp.float32, least / len(shards), largest / len(shards)))
        level = level * jnp.repeat(steps, dims[axis_at] // blocks).reshape([-1 if axis == axis_at else 1 for axis in range(len(dims))])
    return level


def noise(key, extent, deviation, reach, cuts=(), dtype=jnp.bfloat16):
    entries = jax.random.normal(key, extent, jnp.float32) * deviation
    if len(cuts) > 0:
        entries = levels(key, extent, cuts, -0.22, 0.18) * entries
    return jnp.clip(entries, min=-reach, max=reach).astype(dtype)


def setup_inputs(seed: int = 0) -> dict:
    seeds = jax.random.split(jax.random.key(seed), 11)
    return {
        "queries": draw_queries(jax.random.fold_in(seeds[10], 71), 0),
        "rollout_suffix_keys": draw_rollout_suffix_keys(jax.random.fold_in(seeds[10], 71), 0),
        "rollout_suffix_values": noise(seeds[2], (SUFFIX_TOTAL, LOCAL_KV_HEADS * HEAD_WIDTH), 1.0, 6.0, ((0, 64), (1, 4))),
        "blockwise_prefix_keys": noise(seeds[3], (PREFIX_TOKENS, LOCAL_KV_HEADS * HEAD_WIDTH), 1.0, 6.0, ((0, 64), (1, 4))),
        "blockwise_prefix_values": noise(seeds[4], (PREFIX_TOKENS, LOCAL_KV_HEADS * HEAD_WIDTH), 1.0, 6.0, ((0, 64), (1, 4))),
        "block_prompt": draw_block_prompt(jax.random.fold_in(seeds[10], 71), 0),
        "rollout_prompt": draw_rollout_prompt(jax.random.fold_in(seeds[10], 71), 0),
        "suffix_length": draw_suffix_length(jax.random.fold_in(seeds[10], 71), 0),
        "out_weight": noise(seeds[8], (LOCAL_Q_HEADS * HEAD_WIDTH, D), (LOCAL_Q_HEADS * HEAD_WIDTH) ** -0.5, 0.09375, ((0, 4),)),
        "out_grad": noise(seeds[9], (SUFFIX_TOTAL, D), 1.0, 6.0, ((0, 64), (1, 4))),
    }


def rounded(value_entries):
    return lax.optimization_barrier(value_entries.astype(jnp.bfloat16)).astype(jnp.float32)


def reference(queries, rollout_suffix_keys, rollout_suffix_values, blockwise_prefix_keys, blockwise_prefix_values, block_prompt, rollout_prompt, suffix_length, out_weight, out_grad):
    group_stride = LOCAL_Q_HEADS // LOCAL_KV_HEADS
    score_scale = HEAD_WIDTH ** -0.5
    prompt_stride = PREFIX_BLOCKS // PROMPTS
    prefix_row_piece = prompt_stride * BLOCK_TOKENS
    block_order = jnp.argsort(block_prompt, stable=True).astype(jnp.int32)
    query_head_rows = queries.reshape(ROLLOUT_COUNT, SUFFIX_SLOTS, LOCAL_KV_HEADS, group_stride, HEAD_WIDTH)
    suffix_key_grouped = rollout_suffix_keys.reshape(ROLLOUT_COUNT, SUFFIX_SLOTS, LOCAL_KV_HEADS, HEAD_WIDTH)
    suffix_value_grouped = rollout_suffix_values.reshape(ROLLOUT_COUNT, SUFFIX_SLOTS, LOCAL_KV_HEADS, HEAD_WIDTH)
    prefix_key_piece = blockwise_prefix_keys.reshape(PREFIX_BLOCKS, BLOCK_TOKENS, LOCAL_KV_HEADS, HEAD_WIDTH)
    prefix_value_piece = blockwise_prefix_values.reshape(PREFIX_BLOCKS, BLOCK_TOKENS, LOCAL_KV_HEADS, HEAD_WIDTH)
    positions = jnp.arange(SUFFIX_SLOTS)
    live_rows = (positions[None, :] < suffix_length[:, None]).astype(jnp.float32)

    def gather_keys(group_member):
        selected_blocks = lax.dynamic_slice_in_dim(block_order, rollout_prompt[group_member] * prompt_stride, prompt_stride).astype(jnp.int32)
        gathered_key_rows = jnp.concatenate([prefix_key_piece[selected_blocks].reshape(prefix_row_piece, LOCAL_KV_HEADS, HEAD_WIDTH), suffix_key_grouped[group_member]], 0)
        gathered_value_rows = jnp.concatenate([prefix_value_piece[selected_blocks].reshape(prefix_row_piece, LOCAL_KV_HEADS, HEAD_WIDTH), suffix_value_grouped[group_member]], 0)
        causal = (positions[:, None] >= positions[None, :]) & (positions[None, :] < suffix_length[group_member])
        visible_mask = jnp.concatenate([jnp.ones((SUFFIX_SLOTS, prefix_row_piece), bool), causal], 1)
        return selected_blocks, gathered_key_rows, gathered_value_rows, visible_mask

    def masked_logits(query_rows, gathered_key_rows, visible_mask):
        logits = jnp.einsum('sged,kgd->sgek', query_rows.astype(jnp.float32), gathered_key_rows.astype(jnp.float32)) * score_scale
        return jnp.where(visible_mask[:, None, None, :], logits, -jnp.inf)

    def forward(group_member):
        selected_blocks, gathered_key_rows, gathered_value_rows, visible_mask = gather_keys(group_member)
        logits = masked_logits(query_head_rows[group_member], gathered_key_rows, visible_mask)
        peak = jnp.max(logits, -1)
        weights = jnp.exp(logits - peak[..., None])
        weight_sum = jnp.sum(weights, -1)
        accum = jnp.einsum('sgek,kgd->sged', rounded(weights), gathered_value_rows.astype(jnp.float32))
        output = accum / weight_sum[..., None] * live_rows[group_member][:, None, None, None]
        return output.astype(jnp.bfloat16), peak + jnp.log(weight_sum)

    attended, log_total = lax.map(forward, jnp.arange(ROLLOUT_COUNT))
    projected = jnp.dot(attended.reshape(SUFFIX_TOTAL, LOCAL_Q_HEADS * HEAD_WIDTH), out_weight, preferred_element_type=jnp.float32).astype(jnp.bfloat16)
    attended_gradient = jnp.dot(out_grad, out_weight.T, preferred_element_type=jnp.float32) * live_rows.reshape(SUFFIX_TOTAL)[:, None]
    attended_gradient = attended_gradient.astype(jnp.bfloat16).reshape(ROLLOUT_COUNT, SUFFIX_SLOTS, LOCAL_KV_HEADS, group_stride, HEAD_WIDTH)

    def backward(running, group_member):
        prefix_key_gradient, prefix_value_gradient = running
        selected_blocks, gathered_key_rows, gathered_value_rows, visible_mask = gather_keys(group_member)
        query_rows = query_head_rows[group_member].astype(jnp.float32)
        logits = masked_logits(query_head_rows[group_member], gathered_key_rows, visible_mask)
        probs = jnp.exp(logits - log_total[group_member][..., None])
        d_rows = attended_gradient[group_member].astype(jnp.float32)
        row_dots = jnp.sum(d_rows * attended[group_member].astype(jnp.float32), -1)
        d_probs = jnp.einsum('sged,kgd->sgek', d_rows, gathered_value_rows.astype(jnp.float32))
        d_logits = rounded(probs * (d_probs - row_dots[..., None]))
        dq_rows = jnp.einsum('sgek,kgd->sged', d_logits, gathered_key_rows.astype(jnp.float32)) * score_scale
        key_row_gradient = jnp.einsum('sgek,sged->kgd', d_logits, query_rows) * score_scale
        value_row_gradient = jnp.einsum('sgek,sged->kgd', rounded(probs), d_rows)
        prefix_key_gradient = prefix_key_gradient.at[selected_blocks].add(key_row_gradient[:prefix_row_piece].reshape(prompt_stride, BLOCK_TOKENS, LOCAL_KV_HEADS, HEAD_WIDTH))
        prefix_value_gradient = prefix_value_gradient.at[selected_blocks].add(value_row_gradient[:prefix_row_piece].reshape(prompt_stride, BLOCK_TOKENS, LOCAL_KV_HEADS, HEAD_WIDTH))
        return (prefix_key_gradient, prefix_value_gradient), (dq_rows, key_row_gradient[prefix_row_piece:], value_row_gradient[prefix_row_piece:])

    blank_buffer = jnp.zeros((PREFIX_BLOCKS, BLOCK_TOKENS, LOCAL_KV_HEADS, HEAD_WIDTH), jnp.float32)
    (prefix_key_gradient, prefix_value_gradient), (dq_all, suffix_key_gradient, suffix_value_gradient) = lax.scan(backward, (blank_buffer, blank_buffer), jnp.arange(ROLLOUT_COUNT))
    return (projected,
            dq_all.reshape(SUFFIX_TOTAL, LOCAL_Q_HEADS * HEAD_WIDTH).astype(jnp.bfloat16),
            suffix_key_gradient.reshape(SUFFIX_TOTAL, LOCAL_KV_HEADS * HEAD_WIDTH).astype(jnp.bfloat16),
            suffix_value_gradient.reshape(SUFFIX_TOTAL, LOCAL_KV_HEADS * HEAD_WIDTH).astype(jnp.bfloat16),
            prefix_key_gradient.reshape(PREFIX_TOKENS, LOCAL_KV_HEADS * HEAD_WIDTH).astype(jnp.bfloat16),
            prefix_value_gradient.reshape(PREFIX_TOKENS, LOCAL_KV_HEADS * HEAD_WIDTH).astype(jnp.bfloat16))
```

```python
import functools

import jax
import jax.numpy as jnp
from jax import lax
from jax.experimental import pallas as pl
from jax.experimental.pallas import tpu as pltpu
from jax.sharding import PartitionSpec as P

HEAD_WIDTH = 128
PROMPTS = 8
F32 = jnp.float32
BF16 = jnp.bfloat16
NT = (((1,), (1,)), ((), ()))
VMEM_LIMIT = 56 * 1024 * 1024


def dot(a, b):
    return jnp.dot(a, b, preferred_element_type=F32)


def dot_nt(a, b):
    return lax.dot_general(a, b, NT, preferred_element_type=F32)


def iota(shape, dim):
    return lax.broadcasted_iota(jnp.int32, shape, dim)


def select_kernel(pieces_ref, picked_ref, map_ref, *, blocks, per_prompt, width):
    meta = pieces_ref[:, width : width + 128].astype(F32)
    block_prompt, rollout_prompt = meta[:, 0:1], meta[:, 1:2]
    lanes = iota((blocks, 128), 1).astype(F32)
    one_hot = (block_prompt == lanes).astype(BF16)
    same = dot_nt(one_hot, one_hot)
    row, col = iota((blocks, blocks), 0), iota((blocks, blocks), 1)
    rank = jnp.sum(jnp.where(col < row, same, 0.0), axis=1, keepdims=True)
    code_col = block_prompt * per_prompt + rank
    code_row = jnp.sum(jnp.where(row == col, code_col, 0.0), axis=0, keepdims=True)
    wants = blocks * per_prompt
    expand = (iota((wants, blocks), 0) // per_prompt == iota((wants, blocks), 1)).astype(F32)
    rollout_row = jnp.sum(jnp.where(row == col, rollout_prompt, 0.0), axis=0, keepdims=True)
    want_col = jnp.sum(expand * rollout_row, axis=1, keepdims=True) * per_prompt
    want_col = want_col + (iota((wants, 1), 0) % per_prompt).astype(F32)
    expand_t = (iota((blocks, wants), 1) // per_prompt == iota((blocks, wants), 0)).astype(F32)
    want_row = jnp.sum(expand_t * rollout_prompt, axis=0, keepdims=True) * per_prompt
    want_row = want_row + (iota((1, wants), 1) % per_prompt).astype(F32)
    choose = (want_col == code_row).astype(BF16)
    map_ref[...] = (code_col == want_row).astype(BF16)
    picked_ref[...] = dot(choose, pieces_ref[:, :width]).astype(BF16)


def combine_kernel(map_ref, terms_ref, out_ref):
    out_ref[...] = dot(map_ref[...], terms_ref[...]).astype(BF16)


def grad_rows_kernel(at_ref, len_ref, g0, g1, g2, g3, w_ref, rows_ref, cols_ref, acc):
    step = pl.program_id(0)
    for d, g in enumerate((g0, g1, g2, g3)):

        @pl.when(step == d)
        def _():
            term = dot_nt(w_ref[...], g[...])
            acc[...] = term if d == 0 else acc[...] + term

    @pl.when(step == 3)
    def _():
        total = acc[...]
        live = iota(total.shape, 1) < len_ref[0]
        total = jnp.where(live, total, 0.0)
        cols_ref[...] = total.astype(BF16)
        for h in range(total.shape[0] // HEAD_WIDTH):
            part = slice(h * HEAD_WIDTH, (h + 1) * HEAD_WIDTH)
            rows_ref[:, part] = total[part].T.astype(BF16)


def project_kernel(at_ref, a_ref, w_ref, o0, o1, o2, o3):
    step = pl.program_id(0)
    for d, o in enumerate((o0, o1, o2, o3)):

        @pl.when(step == d)
        def _():
            o[...] = dot(a_ref[...], w_ref[...]).astype(o.dtype)


def attention_kernel(
    len_ref,
    q_ref,
    ks_ref,
    vs_ref,
    g_ref,
    da_ref,
    dat_ref,
    att_ref,
    dq_ref,
    dks_ref,
    dvs_ref,
    dg_ref,
    k_all,
    v_all,
    dk_acc,
    dv_acc,
    *,
    scale,
):
    n = len_ref[0]
    pieces, width = g_ref.shape
    parts = width // 256
    suffix = ks_ref.shape[0]
    prefix = pieces * parts
    for t in range(parts):
        rows = slice(t * pieces, (t + 1) * pieces)
        k_all[rows, :] = g_ref[:, t * 128 : (t + 1) * 128]
        v_all[rows, :] = g_ref[:, (parts + t) * 128 : (parts + t + 1) * 128]
    k_all[prefix:, :] = ks_ref[...]
    v_all[prefix:, :] = vs_ref[...]
    k_t = k_all[...].T
    v_t = v_all[...].T
    heads = q_ref.shape[1] // 128
    key_at = iota((suffix, 2 * suffix), 0)
    slot_at = iota((suffix, 2 * suffix), 1) % suffix
    hidden = jnp.logical_or(key_at > slot_at, key_at >= n)
    live = iota((1, 2 * suffix), 1) % suffix < n
    to_log2 = scale * 1.4426950408889634
    for pair in range(heads // 2):
        one = slice(pair * 256, pair * 256 + 128)
        two = slice(pair * 256 + 128, pair * 256 + 256)
        q2 = jnp.concatenate([q_ref[:, one], q_ref[:, two]], axis=0)
        da2 = jnp.concatenate([da_ref[:, one], da_ref[:, two]], axis=0)
        dat2 = jnp.concatenate([dat_ref[one, :], dat_ref[two, :]], axis=1)
        s_pre = dot_nt(k_all[:prefix], q2)
        s_suf = jnp.where(hidden, -jnp.inf, dot_nt(k_all[prefix:], q2))
        peak = jnp.maximum(
            jnp.max(s_pre, axis=0, keepdims=True), jnp.max(s_suf, axis=0, keepdims=True)
        )
        w = jnp.concatenate(
            [jnp.exp2((s_pre - peak) * to_log2), jnp.exp2((s_suf - peak) * to_log2)], axis=0
        )
        inverse = 1.0 / jnp.sum(w, axis=0, keepdims=True)
        out_t = dot(v_t, w.astype(BF16)) * inverse
        out_t = jnp.where(live, out_t, 0.0).astype(BF16).astype(F32)
        att_ref[:, one] = out_t[:, :128].T.astype(BF16)
        att_ref[:, two] = out_t[:, 128:].T.astype(BF16)
        dots = jnp.sum(out_t * dat2.astype(F32), axis=0, keepdims=True)
        probs = w * inverse
        ds = (probs * (dot(v_all[...], dat2) - dots)).astype(BF16)
        dq_t = dot(k_t, ds) * scale
        dq_ref[:, one] = dq_t[:, :128].T.astype(BF16)
        dq_ref[:, two] = dq_t[:, 128:].T.astype(BF16)
        dk = dot(ds, q2)
        dv = dot(probs.astype(BF16), da2)
        if pair == 0:
            dk_acc[...] = dk
            dv_acc[...] = dv
        else:
            dk_acc[...] += dk
            dv_acc[...] += dv
    for t in range(parts):
        rows = slice(t * pieces, (t + 1) * pieces)
        dg_ref[:, t * 128 : (t + 1) * 128] = (dk_acc[rows] * scale).astype(BF16)
        dg_ref[:, (parts + t) * 128 : (parts + t + 1) * 128] = dv_acc[rows].astype(BF16)
    dks_ref[...] = (dk_acc[prefix:] * scale).astype(BF16)
    dvs_ref[...] = dv_acc[prefix:].astype(BF16)


def whole(memory=pltpu.VMEM):
    return pl.BlockSpec(memory_space=memory)


def params():
    return pltpu.CompilerParams(vmem_limit_bytes=VMEM_LIMIT)


def shape(*dims, dtype=BF16):
    return jax.ShapeDtypeStruct(dims, dtype)


def shards(
    queries,
    suffix_keys,
    suffix_values,
    prefix_keys,
    prefix_values,
    block_prompt,
    rollout_prompt,
    suffix_length,
    out_weight,
    out_grad,
):
    homes = lax.axis_size("seq")
    cuts = lax.axis_size("tensor")
    rows, width = queries.shape
    features = out_grad.shape[1]
    per_prompt = homes // PROMPTS
    tokens = prefix_keys.shape[0] // homes
    piece = 2 * tokens * HEAD_WIDTH
    at = lax.axis_index("tensor").astype(jnp.int32).reshape(1)

    parts = [p[t * homes : (t + 1) * homes] for p in (prefix_keys, prefix_values) for t in range(tokens)]
    lane = iota((homes, 128), 1)
    meta = jnp.where(lane == 0, block_prompt[0], jnp.where(lane == 1, rollout_prompt[0], 0))
    sent = jnp.concatenate(parts + [meta.astype(BF16)], axis=1)
    pieces = lax.all_to_all(sent, "seq", 0, 0, tiled=True)
    picked, home_map = pl.pallas_call(
        functools.partial(select_kernel, blocks=homes, per_prompt=per_prompt, width=piece),
        out_shape=(shape(homes * per_prompt, piece), shape(homes, homes * per_prompt)),
        in_specs=[whole()],
        out_specs=(whole(), whole()),
        compiler_params=params(),
        name="select",
    )(pieces)
    gathered = lax.all_to_all(
        picked.reshape(homes, per_prompt, piece), "seq", 0, 0, tiled=True
    ).reshape(homes * per_prompt, piece)

    turn = lambda x, d: lax.ppermute(x, "tensor", [(i, (i + d) % cuts) for i in range(cuts)])
    grads = [out_grad] + [turn(out_grad, cuts - d) for d in range(1, cuts)]
    weight_spec = pl.BlockSpec(
        (width, features), lambda d, at_ref, *_: (0, lax.rem(at_ref[0] + d, cuts))
    )
    d_rows, d_cols = pl.pallas_call(
        grad_rows_kernel,
        out_shape=(shape(rows, width), shape(width, rows)),
        grid_spec=pltpu.PrefetchScalarGridSpec(
            num_scalar_prefetch=2,
            grid=(cuts,),
            in_specs=[whole()] * cuts + [weight_spec],
            out_specs=(whole(), whole()),
            scratch_shapes=[pltpu.VMEM((width, rows), F32)],
        ),
        compiler_params=params(),
        name="grad_rows",
    )(at, suffix_length, *grads, out_weight)

    keys = prefix_keys.shape[0] * per_prompt + rows
    attended, d_queries, d_suffix_keys, d_suffix_values, d_gathered = pl.pallas_call(
        functools.partial(attention_kernel, scale=HEAD_WIDTH**-0.5),
        out_shape=(
            shape(rows, width),
            shape(rows, width),
            shape(rows, HEAD_WIDTH),
            shape(rows, HEAD_WIDTH),
            shape(homes * per_prompt, piece),
        ),
        in_specs=[whole(pltpu.SMEM)] + [whole()] * 6,
        out_specs=(whole(),) * 5,
        scratch_shapes=[
            pltpu.VMEM((keys, HEAD_WIDTH), BF16),
            pltpu.VMEM((keys, HEAD_WIDTH), BF16),
            pltpu.VMEM((keys, HEAD_WIDTH), F32),
            pltpu.VMEM((keys, HEAD_WIDTH), F32),
        ],
        compiler_params=params(),
        name="attention",
    )(suffix_length, queries, suffix_keys, suffix_values, gathered, d_rows, d_cols)

    head_terms = pl.pallas_call(
        project_kernel,
        out_shape=(shape(rows, features, dtype=F32),) + (shape(rows, features),) * (cuts - 1),
        grid_spec=pltpu.PrefetchScalarGridSpec(
            num_scalar_prefetch=1,
            grid=(cuts,),
            in_specs=[whole(), weight_spec],
            out_specs=(whole(),) * cuts,
        ),
        compiler_params=params(),
        name="project",
    )(at, attended, out_weight)
    projected = head_terms[0]
    for d in range(1, cuts):
        projected = projected + turn(head_terms[d], d).astype(F32)

    terms = lax.all_to_all(
        d_gathered.reshape(homes, per_prompt, piece), "seq", 0, 0, tiled=True
    ).reshape(homes * per_prompt, piece)
    sums = pl.pallas_call(
        combine_kernel,
        out_shape=shape(homes, piece),
        in_specs=[whole(), whole()],
        out_specs=whole(),
        compiler_params=params(),
        name="combine",
    )(home_map, terms)
    back = lax.all_to_all(sums, "seq", 0, 0, tiled=True)
    back = [back[:, t * HEAD_WIDTH : (t + 1) * HEAD_WIDTH] for t in range(2 * tokens)]
    d_prefix_keys = jnp.concatenate(back[:tokens], axis=0)
    d_prefix_values = jnp.concatenate(back[tokens:], axis=0)
    return (
        projected.astype(BF16),
        d_queries,
        d_suffix_keys,
        d_suffix_values,
        d_prefix_keys,
        d_prefix_values,
    )


def solution(mesh):
    split = P("seq", "tensor")
    in_specs = (split,) * 5 + (P("seq"),) * 3 + (P("tensor", None), split)
    return jax.shard_map(
        shards, mesh=mesh, in_specs=in_specs, out_specs=(split,) * 6, check_vma=False
    )
```

```python
import functools

import jax
import jax.numpy as jnp
from jax import lax
from jax.experimental import pallas as pl
from jax.experimental.pallas import tpu as pltpu
from jax.sharding import PartitionSpec as P

HEAD_WIDTH = 128
PROMPTS = 8
F32 = jnp.float32
BF16 = jnp.bfloat16
NT = (((1,), (1,)), ((), ()))


def dot(a, b):
    return jnp.dot(a, b, preferred_element_type=F32)


def dot_nt(a, b):
    return lax.dot_general(a, b, NT, preferred_element_type=F32)


def iota(shape, dim):
    return lax.broadcasted_iota(jnp.int32, shape, dim)


def one_hot(left, right):
    return (left == right).astype(BF16)


def fiota(shape, dim):
    return iota(shape, dim).astype(F32)


def pack_kernel(block_ref, rollout_ref, keys_ref, values_ref, sent_ref, *, rows):
    total, tall = keys_ref.shape[0], sent_ref.shape[0]
    group = rows + 2
    row, col = iota((tall, total), 0), iota((tall, total), 1)
    place = row % group
    source = jnp.where(place < rows, (row // group) * rows + place, -1)
    packed = dot(one_hot(source, col), keys_ref[...])
    packed = packed + dot(one_hot(source - total, col), values_ref[...])
    row, lane = iota(packed.shape, 0), iota(packed.shape, 1)
    names = jnp.where(lane == 0, block_ref[0], jnp.where(lane == 1, rollout_ref[0], 0))
    packed = jnp.where(row % group == rows, names.astype(F32), packed)
    sent_ref[...] = packed.astype(BF16)


def block_codes(pieces, *, blocks, per_prompt, group):
    tall = pieces.shape[0]
    take = one_hot(iota((blocks, tall), 0) * group + group - 2, iota((blocks, tall), 1))
    meta = dot(take, pieces)
    block_prompt, rollout_prompt = meta[:, 0:1], meta[:, 1:2]
    named = one_hot(block_prompt, fiota((blocks, 128), 1))
    same = dot_nt(named, named)
    row, col = iota((blocks, blocks), 0), iota((blocks, blocks), 1)
    rank = jnp.sum(jnp.where(col < row, same, 0.0), axis=1, keepdims=True)
    return block_prompt * per_prompt + rank, rollout_prompt, meta


def select_kernel(pieces_ref, picked_ref, *, blocks, per_prompt, rows):
    group = rows + 2
    pieces = pieces_ref[...]
    code, _, meta = block_codes(pieces, blocks=blocks, per_prompt=per_prompt, group=group)
    tall, wants = pieces.shape[0], picked_ref.shape[0]
    span = per_prompt * rows
    spread = iota((blocks, tall), 1) // group == iota((blocks, tall), 0)
    have = jnp.sum(jnp.where(spread, code, 0.0), axis=0, keepdims=True) * rows
    place = iota((1, tall), 1) % group
    have = jnp.where(place < rows, have + place.astype(F32), -1.0)
    expand = one_hot(iota((wants, blocks), 0) // span, iota((wants, blocks), 1))
    want = dot(expand, meta.astype(BF16))[:, 1:2] * span
    want = want + (iota((wants, 1), 0) % span).astype(F32)
    picked_ref[...] = dot(one_hot(want, have), pieces).astype(BF16)


def map_kernel(pieces_ref, map_ref, *, blocks, per_prompt, rows):
    code, rollout, _ = block_codes(
        pieces_ref[...], blocks=blocks, per_prompt=per_prompt, group=rows + 2
    )
    tall, wants = map_ref.shape
    span = per_prompt * rows
    row, col = iota((tall, blocks), 0), iota((tall, blocks), 1)
    eye = iota((blocks, blocks), 0) == iota((blocks, blocks), 1)
    code_row = jnp.sum(jnp.where(eye, code, 0.0), axis=0, keepdims=True)
    have = jnp.sum(jnp.where(row // rows == col, code_row, 0.0), axis=1, keepdims=True) * rows
    have = have + (iota((tall, 1), 0) % rows).astype(F32)
    spread = iota((blocks, wants), 1) // span == iota((blocks, wants), 0)
    want = jnp.sum(jnp.where(spread, rollout, 0.0), axis=0, keepdims=True) * span
    want = want + (iota((1, wants), 1) % span).astype(F32)
    map_ref[...] = one_hot(have, want)


def combine_kernel(map_ref, terms_ref, out_ref):
    out_ref[...] = dot(map_ref[...], terms_ref[...]).astype(BF16)


def turned(at_ref, d, cuts, width):
    return pl.ds(pl.multiple_of(lax.rem(at_ref[0] + d, cuts) * width, width), width)


def grad_rows_kernel(at_ref, len_ref, *refs):
    *g_refs, w_ref, rows_ref, cols_ref = refs
    cuts, width = len(g_refs), g_refs[0].shape[1]
    total = None
    for d, g in enumerate(g_refs):
        term = dot_nt(w_ref[:, turned(at_ref, d, cuts, width)], g[...])
        total = term if total is None else total + term
    live = iota(total.shape, 1) < len_ref[0]
    total = jnp.where(live, total, 0.0)
    cols_ref[...] = total.astype(BF16)
    for h in range(total.shape[0] // HEAD_WIDTH):
        part = slice(h * HEAD_WIDTH, (h + 1) * HEAD_WIDTH)
        rows_ref[:, part] = total[part].T.astype(BF16)


def project_kernel(at_ref, a_ref, w_ref, *out_refs):
    cuts, width = len(out_refs), out_refs[0].shape[1]
    for d, o in enumerate(out_refs):
        o[...] = dot(a_ref[...], w_ref[:, turned(at_ref, d, cuts, width)]).astype(o.dtype)


def attention_kernel(
    len_ref,
    q_ref,
    ks_ref,
    vs_ref,
    g_ref,
    da_ref,
    dat_ref,
    att_ref,
    dq_ref,
    dks_ref,
    dvs_ref,
    dg_ref,
    k_all,
    v_all,
    dk_acc,
    dv_acc,
    *,
    scale,
):
    n = len_ref[0]
    half = g_ref.shape[0] // 2
    prefix = half * g_ref.shape[1]
    suffix = ks_ref.shape[0]
    k_all[:prefix, :] = g_ref[:half].reshape(prefix, HEAD_WIDTH)
    v_all[:prefix, :] = g_ref[half:].reshape(prefix, HEAD_WIDTH)
    k_all[prefix:, :] = ks_ref[...]
    v_all[prefix:, :] = vs_ref[...]
    k_t = k_all[...].T
    v_t = v_all[...].T
    heads = q_ref.shape[1] // 128
    key_at = iota((suffix, 2 * suffix), 0)
    slot_at = iota((suffix, 2 * suffix), 1) % suffix
    hidden = jnp.logical_or(key_at > slot_at, key_at >= n)
    live = iota((1, 2 * suffix), 1) % suffix < n
    to_log2 = scale * 1.4426950408889634
    for pair in range(heads // 2):
        one = slice(pair * 256, pair * 256 + 128)
        two = slice(pair * 256 + 128, pair * 256 + 256)
        q2 = jnp.concatenate([q_ref[:, one], q_ref[:, two]], axis=0)
        da2 = jnp.concatenate([da_ref[:, one], da_ref[:, two]], axis=0)
        dat2 = jnp.concatenate([dat_ref[one, :], dat_ref[two, :]], axis=1)
        s_pre = dot_nt(k_all[:prefix], q2)
        s_suf = jnp.where(hidden, -jnp.inf, dot_nt(k_all[prefix:], q2))
        peak = jnp.maximum(
            jnp.max(s_pre, axis=0, keepdims=True), jnp.max(s_suf, axis=0, keepdims=True)
        )
        w = jnp.concatenate(
            [jnp.exp2((s_pre - peak) * to_log2), jnp.exp2((s_suf - peak) * to_log2)], axis=0
        )
        inverse = 1.0 / jnp.sum(w, axis=0, keepdims=True)
        out_t = dot(v_t, w.astype(BF16)) * inverse
        out_t = jnp.where(live, out_t, 0.0).astype(BF16).astype(F32)
        att_ref[:, one] = out_t[:, :128].T.astype(BF16)
        att_ref[:, two] = out_t[:, 128:].T.astype(BF16)
        dots = jnp.sum(out_t * dat2.astype(F32), axis=0, keepdims=True)
        probs = w * inverse
        ds = (probs * (dot(v_all[...], dat2) - dots)).astype(BF16)
        dq_t = dot(k_t, ds) * scale
        dq_ref[:, one] = dq_t[:, :128].T.astype(BF16)
        dq_ref[:, two] = dq_t[:, 128:].T.astype(BF16)
        dk = dot(ds, q2)
        dv = dot(probs.astype(BF16), da2)
        if pair == 0:
            dk_acc[...] = dk
            dv_acc[...] = dv
        else:
            dk_acc[...] += dk
            dv_acc[...] += dv
    dg_ref[:half] = (dk_acc[:prefix] * scale).astype(BF16).reshape(half, -1, HEAD_WIDTH)
    dg_ref[half:] = dv_acc[:prefix].astype(BF16).reshape(half, -1, HEAD_WIDTH)
    dks_ref[...] = (dk_acc[prefix:] * scale).astype(BF16)
    dvs_ref[...] = dv_acc[prefix:].astype(BF16)


def whole(memory=pltpu.VMEM):
    return pl.BlockSpec(memory_space=memory)


def params(mib=24):
    return pltpu.CompilerParams(vmem_limit_bytes=mib * 1024 * 1024)


def shape(*dims, dtype=BF16):
    return jax.ShapeDtypeStruct(dims, dtype)


def shards(
    queries,
    suffix_keys,
    suffix_values,
    prefix_keys,
    prefix_values,
    block_prompt,
    rollout_prompt,
    suffix_length,
    out_weight,
    out_grad,
):
    homes = lax.axis_size("seq")
    cuts = lax.axis_size("tensor")
    rows, width = queries.shape
    features = out_grad.shape[1]
    per_prompt = homes // PROMPTS
    prefix_rows = prefix_keys.shape[0]
    served = 2 * prefix_rows // homes
    group = served + 2
    span = per_prompt * served
    at = lax.axis_index("tensor").astype(jnp.int32).reshape(1)

    sent = pl.pallas_call(
        functools.partial(pack_kernel, rows=served),
        out_shape=shape(homes * group, HEAD_WIDTH),
        in_specs=[whole(pltpu.SMEM)] * 2 + [whole()] * 2,
        out_specs=whole(),
        compiler_params=params(),
        name="pack",
    )(block_prompt, rollout_prompt, prefix_keys, prefix_values)
    pieces = lax.all_to_all(
        sent.reshape(homes, group // 2, 2, HEAD_WIDTH), "seq", 0, 0, tiled=True
    ).reshape(homes * group, HEAD_WIDTH)
    sizes = dict(blocks=homes, per_prompt=per_prompt, rows=served)
    picked = pl.pallas_call(
        functools.partial(select_kernel, **sizes),
        out_shape=shape(homes * span, HEAD_WIDTH),
        in_specs=[whole()],
        out_specs=whole(),
        compiler_params=params(),
        name="select",
    )(pieces)
    gathered = lax.all_to_all(
        picked.reshape(homes, span, HEAD_WIDTH), "seq", 0, 0, tiled=True
    )
    home_map = pl.pallas_call(
        functools.partial(map_kernel, **sizes),
        out_shape=shape(homes * served, homes * span),
        in_specs=[whole()],
        out_specs=whole(),
        compiler_params=params(),
        name="home_map",
    )(pieces)

    turn = lambda x, d: lax.ppermute(x, "tensor", [(i, (i + d) % cuts) for i in range(cuts)])
    grads = [out_grad] + [turn(out_grad, cuts - d) for d in range(1, cuts)]
    d_rows, d_cols = pl.pallas_call(
        grad_rows_kernel,
        out_shape=(shape(rows, width), shape(width, rows)),
        in_specs=[whole(pltpu.SMEM)] * 2 + [whole()] * (cuts + 1),
        out_specs=(whole(), whole()),
        compiler_params=params(),
        name="grad_rows",
    )(at, suffix_length, *grads, out_weight)

    keys = prefix_keys.shape[0] * per_prompt + rows
    attended, d_queries, d_suffix_keys, d_suffix_values, d_gathered = pl.pallas_call(
        functools.partial(attention_kernel, scale=HEAD_WIDTH**-0.5),
        out_shape=(
            shape(rows, width),
            shape(rows, width),
            shape(rows, HEAD_WIDTH),
            shape(rows, HEAD_WIDTH),
            shape(homes, span, HEAD_WIDTH),
        ),
        in_specs=[whole(pltpu.SMEM)] + [whole()] * 6,
        out_specs=(whole(),) * 5,
        scratch_shapes=[
            pltpu.VMEM((keys, HEAD_WIDTH), BF16),
            pltpu.VMEM((keys, HEAD_WIDTH), BF16),
            pltpu.VMEM((keys, HEAD_WIDTH), F32),
            pltpu.VMEM((keys, HEAD_WIDTH), F32),
        ],
        compiler_params=params(),
        name="attention",
    )(suffix_length, queries, suffix_keys, suffix_values, gathered, d_rows, d_cols)

    head_terms = pl.pallas_call(
        project_kernel,
        out_shape=(shape(rows, features, dtype=F32),) + (shape(rows, features),) * (cuts - 1),
        in_specs=[whole(pltpu.SMEM), whole(), whole()],
        out_specs=(whole(),) * cuts,
        compiler_params=params(),
        name="project",
    )(at, attended, out_weight)
    projected = head_terms[0]
    for d in range(1, cuts):
        projected = projected + turn(head_terms[d], d).astype(F32)

    terms = lax.all_to_all(d_gathered, "seq", 0, 0, tiled=True)
    sums = pl.pallas_call(
        combine_kernel,
        out_shape=shape(homes * served, HEAD_WIDTH),
        in_specs=[whole(), whole()],
        out_specs=whole(),
        compiler_params=params(),
        name="combine",
    )(home_map, terms.reshape(homes * span, HEAD_WIDTH))
    back = lax.all_to_all(
        sums.reshape(homes, served, HEAD_WIDTH), "seq", 0, 0, tiled=True
    ).reshape(homes * served, HEAD_WIDTH)
    d_prefix_keys, d_prefix_values = back[:prefix_rows], back[prefix_rows:]
    return (
        projected.astype(BF16),
        d_queries,
        d_suffix_keys,
        d_suffix_values,
        d_prefix_keys,
        d_prefix_values,
    )


def solution(mesh):
    split = P("seq", "tensor")
    in_specs = (split,) * 5 + (P("seq"),) * 3 + (P("tensor", None), split)
    return jax.shard_map(
        shards, mesh=mesh, in_specs=in_specs, out_specs=(split,) * 6, check_vma=False
    )
```

```python
import functools

import jax
import jax.numpy as jnp
from jax import lax
from jax.experimental import pallas as pl
from jax.experimental.pallas import tpu as pltpu
from jax.sharding import PartitionSpec as P

HEAD_WIDTH = 128
PROMPTS = 8
SERVERS = 16
F32 = jnp.float32
BF16 = jnp.bfloat16
NT = (((1,), (1,)), ((), ()))


def dot(a, b):
    return jnp.dot(a, b, preferred_element_type=F32)


def dot_nt(a, b):
    return lax.dot_general(a, b, NT, preferred_element_type=F32)


def iota(shape, dim):
    return lax.broadcasted_iota(jnp.int32, shape, dim)


def one_hot(left, right):
    return (left == right).astype(BF16)


def fiota(shape, dim):
    return iota(shape, dim).astype(F32)


def pack_kernel(block_ref, rollout_ref, keys_ref, values_ref, sent_ref, *, rows):
    total, tall = keys_ref.shape[0], sent_ref.shape[0]
    group = rows + 2
    row, col = iota((tall, total), 0), iota((tall, total), 1)
    place = row % group
    source = jnp.where(place < rows, (row // group) * rows + place, -1)
    packed = dot(one_hot(source, col), keys_ref[...])
    packed = packed + dot(one_hot(source - total, col), values_ref[...])
    row, lane = iota(packed.shape, 0), iota(packed.shape, 1)
    names = jnp.where(lane == 0, block_ref[0], jnp.where(lane == 1, rollout_ref[0], 0))
    packed = jnp.where(row % group >= rows, names.astype(F32), packed)
    sent_ref[...] = packed.astype(BF16)


def swap_pairs(tall, outer):
    row, col = iota((tall, tall), 0), iota((tall, tall), 1)
    pair = row // 2
    return one_hot((pair % outer * (tall // 2 // outer) + pair // outer) * 2 + row % 2, col)


def by_place_kernel(pieces_ref, out_ref, *, servers):
    tall = pieces_ref.shape[0]
    out_ref[...] = dot(swap_pairs(tall, servers), pieces_ref[...]).astype(BF16)


def block_codes(refs, *, blocks, per_prompt, rows):
    each = 2 * blocks // len(refs)
    meta = jnp.concatenate([ref[rows // 2 * each : (rows // 2 + 1) * each] for ref in refs])
    meta = dot(one_hot(iota((blocks, 2 * blocks), 0) * 2, iota((blocks, 2 * blocks), 1)), meta)
    block_prompt = meta[:, 0:1]
    named = one_hot(block_prompt, fiota((blocks, 128), 1))
    same = dot_nt(named, named)
    row, col = iota((blocks, blocks), 0), iota((blocks, blocks), 1)
    rank = jnp.sum(jnp.where(col < row, same, 0.0), axis=1, keepdims=True)
    return block_prompt * per_prompt + rank, meta[: blocks // len(refs), 1:2]


def select_kernel(*refs, blocks, per_prompt, rows):
    *refs, picked_ref = refs
    code, rollout = block_codes(refs, blocks=blocks, per_prompt=per_prompt, rows=rows)
    servers, each = rollout.shape[0], 2 * blocks // len(refs)
    span, wants = 2 * per_prompt, 2 * per_prompt * servers
    spread = iota((blocks, 2 * blocks), 1) // 2 == iota((blocks, 2 * blocks), 0)
    have = jnp.sum(jnp.where(spread, code, 0.0), axis=0, keepdims=True) * 2
    have = have + (iota((1, 2 * blocks), 1) % 2).astype(F32)
    want = jnp.broadcast_to(rollout.reshape(servers, 1, 1), (servers, span, 1))
    want = want.reshape(wants, 1) * span + (iota((wants, 1), 0) % span).astype(F32)
    choose = one_hot(want, have)
    for p in range(rows // 2):
        pieces = jnp.concatenate([ref[p * each : (p + 1) * each] for ref in refs])
        picked = dot(choose, pieces).astype(BF16)
        picked_ref[:, p * span : (p + 1) * span, :] = picked.reshape(servers, span, HEAD_WIDTH)


def map_kernel(*refs, blocks, per_prompt, rows):
    *refs, map_ref = refs
    code, rollout = block_codes(refs, blocks=blocks, per_prompt=per_prompt, rows=rows)
    tall, wants = map_ref.shape
    servers, span = rollout.shape[0], 2 * per_prompt
    eye = iota((blocks, blocks), 0) == iota((blocks, blocks), 1)
    code_row = jnp.sum(jnp.where(eye, code, 0.0), axis=0, keepdims=True)
    mine = iota((tall, blocks), 0) // 2 == iota((tall, blocks), 1)
    have = jnp.sum(jnp.where(mine, code_row, 0.0), axis=1, keepdims=True) * 2
    have = have + (iota((tall, 1), 0) % 2).astype(F32)
    spread = iota((servers, wants), 1) // span == iota((servers, wants), 0)
    want = jnp.sum(jnp.where(spread, rollout, 0.0), axis=0, keepdims=True) * span
    want = want + (iota((1, wants), 1) % span).astype(F32)
    map_ref[...] = one_hot(have, want)


def combine_kernel(map_ref, terms_ref, *out_refs):
    servers, tall, _ = terms_ref.shape
    wants = map_ref.shape[1]
    span, each = wants // servers, map_ref.shape[0] // len(out_refs)
    for p in range(tall // span):
        terms = terms_ref[:, p * span : (p + 1) * span, :].reshape(wants, HEAD_WIDTH)
        sums = dot(map_ref[...], terms)
        for d, ref in enumerate(out_refs):
            ref[p * each : (p + 1) * each, :] = sums[d * each : (d + 1) * each].astype(ref.dtype)


def home_sum_kernel(*refs, servers):
    *refs, out_ref = refs
    total = refs[0][...]
    for ref in refs[1:]:
        total = total + ref[...].astype(F32)
    tall = total.shape[0]
    out_ref[...] = dot(swap_pairs(tall, tall // 2 // servers), total.astype(BF16)).astype(BF16)


def turned(at_ref, d, cuts, width):
    return pl.ds(pl.multiple_of(lax.rem(at_ref[0] + d, cuts) * width, width), width)


def fetch(at_ref, w_ref, held, sems):
    cuts, _, width = held.shape
    copies = [
        pltpu.make_async_copy(w_ref.at[:, turned(at_ref, d, cuts, width)], held.at[d], sems.at[d])
        for d in range(cuts)
    ]
    for copy in copies:
        copy.start()
    return copies


def grad_rows_kernel(at_ref, len_ref, *refs):
    *g_refs, w_ref, rows_ref, cols_ref, held, sems = refs
    total = None
    for d, copy in enumerate(fetch(at_ref, w_ref, held, sems)):
        copy.wait()
        term = dot_nt(held[d], g_refs[d][...])
        total = term if total is None else total + term
    live = iota(total.shape, 1) < len_ref[0]
    total = jnp.where(live, total, 0.0)
    cols_ref[...] = total.astype(BF16)
    for h in range(total.shape[0] // HEAD_WIDTH):
        part = slice(h * HEAD_WIDTH, (h + 1) * HEAD_WIDTH)
        rows_ref[:, part] = total[part].T.astype(BF16)


def project_kernel(at_ref, a_ref, w_ref, *refs):
    *out_refs, held, sems = refs
    for d, copy in enumerate(fetch(at_ref, w_ref, held, sems)):
        copy.wait()
        out_refs[d][...] = dot(a_ref[...], held[d]).astype(out_refs[d].dtype)


def attention_kernel(
    len_ref,
    q_ref,
    ks_ref,
    vs_ref,
    g_ref,
    da_ref,
    dat_ref,
    att_ref,
    dq_ref,
    dks_ref,
    dvs_ref,
    dg_ref,
    k_all,
    v_all,
    dk_acc,
    dv_acc,
    *,
    scale,
):
    n = len_ref[0]
    half = g_ref.shape[0] // 2
    prefix = half * g_ref.shape[1]
    suffix = ks_ref.shape[0]
    k_all[:prefix, :] = g_ref[:half].reshape(prefix, HEAD_WIDTH)
    v_all[:prefix, :] = g_ref[half:].reshape(prefix, HEAD_WIDTH)
    k_all[prefix:, :] = ks_ref[...]
    v_all[prefix:, :] = vs_ref[...]
    k_t = k_all[...].T
    v_t = v_all[...].T
    heads = q_ref.shape[1] // 128
    key_at = iota((suffix, 2 * suffix), 0)
    slot_at = iota((suffix, 2 * suffix), 1) % suffix
    hidden = jnp.logical_or(key_at > slot_at, key_at >= n)
    live = iota((1, 2 * suffix), 1) % suffix < n
    to_log2 = scale * 1.4426950408889634
    for pair in range(heads // 2):
        one = slice(pair * 256, pair * 256 + 128)
        two = slice(pair * 256 + 128, pair * 256 + 256)
        q2 = jnp.concatenate([q_ref[:, one], q_ref[:, two]], axis=0)
        da2 = jnp.concatenate([da_ref[:, one], da_ref[:, two]], axis=0)
        dat2 = jnp.concatenate([dat_ref[one, :], dat_ref[two, :]], axis=1)
        s_pre = dot_nt(k_all[:prefix], q2)
        s_suf = jnp.where(hidden, -jnp.inf, dot_nt(k_all[prefix:], q2))
        peak = jnp.maximum(
            jnp.max(s_pre, axis=0, keepdims=True), jnp.max(s_suf, axis=0, keepdims=True)
        )
        w = jnp.concatenate(
            [jnp.exp2((s_pre - peak) * to_log2), jnp.exp2((s_suf - peak) * to_log2)], axis=0
        )
        inverse = 1.0 / jnp.sum(w, axis=0, keepdims=True)
        out_t = dot(v_t, w.astype(BF16)) * inverse
        out_t = jnp.where(live, out_t, 0.0).astype(BF16).astype(F32)
        att_ref[:, one] = out_t[:, :128].T.astype(BF16)
        att_ref[:, two] = out_t[:, 128:].T.astype(BF16)
        dots = jnp.sum(out_t * dat2.astype(F32), axis=0, keepdims=True)
        probs = w * inverse
        ds = (probs * (dot(v_all[...], dat2) - dots)).astype(BF16)
        dq_t = dot(k_t, ds) * scale
        dq_ref[:, one] = dq_t[:, :128].T.astype(BF16)
        dq_ref[:, two] = dq_t[:, 128:].T.astype(BF16)
        dk = dot(ds, q2)
        dv = dot(probs.astype(BF16), da2)
        if pair == 0:
            dk_acc[...] = dk
            dv_acc[...] = dv
        else:
            dk_acc[...] += dk
            dv_acc[...] += dv
    dg_ref[:half] = (dk_acc[:prefix] * scale).astype(BF16).reshape(half, -1, HEAD_WIDTH)
    dg_ref[half:] = dv_acc[:prefix].astype(BF16).reshape(half, -1, HEAD_WIDTH)
    dks_ref[...] = (dk_acc[prefix:] * scale).astype(BF16)
    dvs_ref[...] = dv_acc[prefix:].astype(BF16)


def whole(memory=pltpu.VMEM):
    return pl.BlockSpec(memory_space=memory)


def params(mib=24):
    return pltpu.CompilerParams(vmem_limit_bytes=mib * 1024 * 1024)


def shape(*dims, dtype=BF16):
    return jax.ShapeDtypeStruct(dims, dtype)


def shards(
    queries,
    suffix_keys,
    suffix_values,
    prefix_keys,
    prefix_values,
    block_prompt,
    rollout_prompt,
    suffix_length,
    out_weight,
    out_grad,
):
    homes = lax.axis_size("seq")
    cuts = lax.axis_size("tensor")
    rows, width = queries.shape
    features = out_grad.shape[1]
    per_prompt = homes // PROMPTS
    prefix_rows = prefix_keys.shape[0]
    served = 2 * prefix_rows // SERVERS
    tall = SERVERS * (served + 2)
    span = per_prompt * served
    groups = [[g + i for i in range(SERVERS)] for g in range(0, homes, SERVERS)]
    at = lax.axis_index("tensor").astype(jnp.int32).reshape(1)

    def swap(x):
        return lax.all_to_all(x, "seq", 0, 0, tiled=True, axis_index_groups=groups)

    def group_turn(x, d):
        to = [(i, (i + d * SERVERS) % homes) for i in range(homes)]
        return lax.ppermute(x, "seq", to)

    sent = pl.pallas_call(
        functools.partial(pack_kernel, rows=served),
        out_shape=shape(tall, HEAD_WIDTH),
        in_specs=[whole(pltpu.SMEM)] * 2 + [whole()] * 2,
        out_specs=whole(),
        compiler_params=params(),
        name="pack",
    )(block_prompt, rollout_prompt, prefix_keys, prefix_values)
    pieces = swap(sent.reshape(SERVERS, served // 2 + 1, 2, HEAD_WIDTH)).reshape(tall, HEAD_WIDTH)
    pieces = pl.pallas_call(
        functools.partial(by_place_kernel, servers=SERVERS),
        out_shape=shape(tall, HEAD_WIDTH),
        in_specs=[whole()],
        out_specs=whole(),
        compiler_params=params(),
        name="by_place",
    )(pieces)
    turns = homes // SERVERS
    pieces = [pieces] + [group_turn(pieces, d) for d in range(1, turns)]
    sizes = dict(blocks=homes, per_prompt=per_prompt, rows=served)
    picked = pl.pallas_call(
        functools.partial(select_kernel, **sizes),
        out_shape=shape(SERVERS, span, HEAD_WIDTH),
        in_specs=[whole()] * turns,
        out_specs=whole(),
        compiler_params=params(),
        name="select",
    )(*pieces)
    gathered = swap(picked)
    home_map = pl.pallas_call(
        functools.partial(map_kernel, **sizes),
        out_shape=shape(2 * homes, 2 * per_prompt * SERVERS),
        in_specs=[whole()] * turns,
        out_specs=whole(),
        compiler_params=params(),
        name="home_map",
    )(*pieces)

    turn = lambda x, d: lax.ppermute(x, "tensor", [(i, (i + d) % cuts) for i in range(cuts)])
    grads = [out_grad] + [turn(out_grad, cuts - d) for d in range(1, cuts)]
    weight = whole(pltpu.HBM)
    held = [
        pltpu.VMEM((cuts, width, features), BF16),
        pltpu.SemaphoreType.DMA((cuts,)),
    ]
    d_rows, d_cols = pl.pallas_call(
        grad_rows_kernel,
        out_shape=(shape(rows, width), shape(width, rows)),
        in_specs=[whole(pltpu.SMEM)] * 2 + [whole()] * cuts + [weight],
        out_specs=(whole(), whole()),
        scratch_shapes=held,
        compiler_params=params(),
        name="grad_rows",
    )(at, suffix_length, *grads, out_weight)

    keys = prefix_keys.shape[0] * per_prompt + rows
    attended, d_queries, d_suffix_keys, d_suffix_values, d_gathered = pl.pallas_call(
        functools.partial(attention_kernel, scale=HEAD_WIDTH**-0.5),
        out_shape=(
            shape(rows, width),
            shape(rows, width),
            shape(rows, HEAD_WIDTH),
            shape(rows, HEAD_WIDTH),
            shape(SERVERS, span, HEAD_WIDTH),
        ),
        in_specs=[whole(pltpu.SMEM)] + [whole()] * 6,
        out_specs=(whole(),) * 5,
        scratch_shapes=[
            pltpu.VMEM((keys, HEAD_WIDTH), BF16),
            pltpu.VMEM((keys, HEAD_WIDTH), BF16),
            pltpu.VMEM((keys, HEAD_WIDTH), F32),
            pltpu.VMEM((keys, HEAD_WIDTH), F32),
        ],
        compiler_params=params(),
        name="attention",
    )(suffix_length, queries, suffix_keys, suffix_values, gathered, d_rows, d_cols)

    head_terms = pl.pallas_call(
        project_kernel,
        out_shape=(shape(rows, features, dtype=F32),) + (shape(rows, features),) * (cuts - 1),
        in_specs=[whole(pltpu.SMEM), whole(), weight],
        out_specs=(whole(),) * cuts,
        scratch_shapes=held,
        compiler_params=params(),
        name="project",
    )(at, attended, out_weight)
    projected = head_terms[0]
    for d in range(1, cuts):
        projected = projected + turn(head_terms[d], d).astype(F32)

    half = SERVERS * served
    sums = pl.pallas_call(
        combine_kernel,
        out_shape=(shape(half, HEAD_WIDTH, dtype=F32),)
        + (shape(half, HEAD_WIDTH),) * (turns - 1),
        in_specs=[whole(), whole()],
        out_specs=(whole(),) * turns,
        compiler_params=params(),
        name="combine",
    )(home_map, swap(d_gathered))
    sums = [sums[0]] + [group_turn(sums[d], turns - d) for d in range(1, turns)]
    home_sums = pl.pallas_call(
        functools.partial(home_sum_kernel, servers=SERVERS),
        out_shape=shape(half, HEAD_WIDTH),
        in_specs=[whole()] * turns,
        out_specs=whole(),
        compiler_params=params(),
        name="home_sum",
    )(*sums)
    back = swap(home_sums.reshape(SERVERS, served, HEAD_WIDTH)).reshape(half, HEAD_WIDTH)
    d_prefix_keys, d_prefix_values = back[:prefix_rows], back[prefix_rows:]
    return (
        projected.astype(BF16),
        d_queries,
        d_suffix_keys,
        d_suffix_values,
        d_prefix_keys,
        d_prefix_values,
    )


def solution(mesh):
    split = P("seq", "tensor")
    in_specs = (split,) * 5 + (P("seq"),) * 3 + (P("tensor", None), split)
    return jax.shard_map(
        shards, mesh=mesh, in_specs=in_specs, out_specs=(split,) * 6, check_vma=False
    )
```

```python
import functools

import jax
import jax.numpy as jnp
from jax import lax
from jax.experimental import pallas as pl
from jax.experimental.pallas import tpu as pltpu
from jax.sharding import PartitionSpec as P

HEAD_WIDTH = 128
PROMPTS = 8
SERVERS = 16
F32 = jnp.float32
BF16 = jnp.bfloat16
NT = (((1,), (1,)), ((), ()))


def dot(a, b):
    return jnp.dot(a, b, preferred_element_type=F32)


def dot_nt(a, b):
    return lax.dot_general(a, b, NT, preferred_element_type=F32)


def iota(shape, dim):
    return lax.broadcasted_iota(jnp.int32, shape, dim)


def one_hot(left, right):
    return (left == right).astype(BF16)


def fiota(shape, dim):
    return iota(shape, dim).astype(F32)


def pack_kernel(block_ref, rollout_ref, keys_ref, values_ref, sent_ref, *, rows, turns):
    total, tall = keys_ref.shape[0], sent_ref.shape[0] // turns
    group = rows + 2
    row, col = iota((tall, total), 0), iota((tall, total), 1)
    place = row % group
    source = jnp.where(place < rows, (row // group) * rows + place, -1)
    packed = dot(one_hot(source, col), keys_ref[...])
    packed = packed + dot(one_hot(source - total, col), values_ref[...])
    row, lane = iota(packed.shape, 0), iota(packed.shape, 1)
    names = jnp.where(lane == 0, block_ref[0], jnp.where(lane == 1, rollout_ref[0], 0))
    packed = jnp.where(row % group >= rows, names.astype(F32), packed).astype(BF16)
    for g in range(turns):
        sent_ref[g * tall : (g + 1) * tall, :] = packed


def swap_pairs(tall, outer):
    row, col = iota((tall, tall), 0), iota((tall, tall), 1)
    pair = row // 2
    return one_hot((pair % outer * (tall // 2 // outer) + pair // outer) * 2 + row % 2, col)


def block_codes(meta, own, *, per_prompt, servers):
    blocks = meta.shape[0]
    block_prompt = meta[:, 0:1].astype(F32)
    named = one_hot(block_prompt, fiota((blocks, 128), 1))
    same = dot_nt(named, named)
    row, col = iota((blocks, blocks), 0), iota((blocks, blocks), 1)
    rank = jnp.sum(jnp.where(col < row, same, 0.0), axis=1, keepdims=True)
    take = one_hot(iota((servers, blocks), 0) + own * servers, iota((servers, blocks), 1))
    return block_prompt * per_prompt + rank, dot(take, meta)[:, 1:2]


def select_kernel(own_ref, pieces_ref, picked_ref, meta_ref, *, per_prompt, servers, rows, turns):
    tall = servers * (rows + 2)
    swap = swap_pairs(tall, servers)
    pieces = [
        dot(swap, pieces_ref[g * tall : (g + 1) * tall]).astype(BF16) for g in range(turns)
    ]
    each, blocks = 2 * servers, servers * turns
    meta = jnp.concatenate([p[rows // 2 * each :] for p in pieces])
    one_each = one_hot(iota((blocks, 2 * blocks), 0) * 2, iota((blocks, 2 * blocks), 1))
    meta = dot(one_each, meta).astype(BF16)
    meta_ref[...] = meta
    code, rollout = block_codes(meta, own_ref[0], per_prompt=per_prompt, servers=servers)
    span, wants = 2 * per_prompt, 2 * per_prompt * servers
    spread = iota((blocks, 2 * blocks), 1) // 2 == iota((blocks, 2 * blocks), 0)
    have = jnp.sum(jnp.where(spread, code, 0.0), axis=0, keepdims=True) * 2
    have = have + (iota((1, 2 * blocks), 1) % 2).astype(F32)
    want = jnp.broadcast_to(rollout.reshape(servers, 1, 1), (servers, span, 1))
    want = want.reshape(wants, 1) * span + (iota((wants, 1), 0) % span).astype(F32)
    choose = one_hot(want, have)
    for p in range(rows // 2):
        from_all = jnp.concatenate([part[p * each : (p + 1) * each] for part in pieces])
        picked = dot(choose, from_all).astype(BF16)
        picked_ref[:, p * span : (p + 1) * span, :] = picked.reshape(servers, span, HEAD_WIDTH)


def map_kernel(own_ref, meta_ref, map_ref, *, per_prompt, servers):
    code, rollout = block_codes(
        meta_ref[...], own_ref[0], per_prompt=per_prompt, servers=servers
    )
    blocks = code.shape[0]
    tall, wants = map_ref.shape
    span = 2 * per_prompt
    eye = iota((blocks, blocks), 0) == iota((blocks, blocks), 1)
    code_row = jnp.sum(jnp.where(eye, code, 0.0), axis=0, keepdims=True)
    mine = iota((tall, blocks), 0) // 2 == iota((tall, blocks), 1)
    have = jnp.sum(jnp.where(mine, code_row, 0.0), axis=1, keepdims=True) * 2
    have = have + (iota((tall, 1), 0) % 2).astype(F32)
    spread = iota((servers, wants), 1) // span == iota((servers, wants), 0)
    want = jnp.sum(jnp.where(spread, rollout, 0.0), axis=0, keepdims=True) * span
    want = want + (iota((1, wants), 1) % span).astype(F32)
    map_ref[...] = one_hot(have, want)


def combine_kernel(map_ref, terms_ref, out_ref, *, turns):
    servers, tall, _ = terms_ref.shape
    wants = map_ref.shape[1]
    span, each = wants // servers, map_ref.shape[0] // turns
    sums = []
    for p in range(tall // span):
        terms = terms_ref[:, p * span : (p + 1) * span, :].reshape(wants, HEAD_WIDTH)
        sums.append(dot(map_ref[...], terms).astype(BF16))
    rows = each * len(sums)
    swap = swap_pairs(rows, len(sums))
    for g in range(turns):
        part = jnp.concatenate([s[g * each : (g + 1) * each] for s in sums])
        out_ref[g * rows : (g + 1) * rows, :] = dot(swap, part).astype(BF16)


def home_sum_kernel(terms_ref, keys_ref, values_ref):
    total = jnp.sum(terms_ref[...].astype(F32), axis=0)
    half = keys_ref.shape[0]
    keys_ref[...] = total[:half].astype(BF16)
    values_ref[...] = total[half:].astype(BF16)


def turned(at_ref, d, cuts, width):
    return pl.ds(pl.multiple_of(lax.rem(at_ref[0] + d, cuts) * width, width), width)


def fetch(at_ref, w_ref, held, sems):
    cuts, _, width = held.shape
    copies = [
        pltpu.make_async_copy(w_ref.at[:, turned(at_ref, d, cuts, width)], held.at[d], sems.at[d])
        for d in range(cuts)
    ]
    for copy in copies:
        copy.start()
    return copies


def grad_rows_kernel(at_ref, len_ref, *refs):
    *g_refs, w_ref, rows_ref, cols_ref, held, sems = refs
    total = None
    for d, copy in enumerate(fetch(at_ref, w_ref, held, sems)):
        copy.wait()
        term = dot_nt(held[d], g_refs[d][...])
        total = term if total is None else total + term
    live = iota(total.shape, 1) < len_ref[0]
    total = jnp.where(live, total, 0.0)
    cols_ref[...] = total.astype(BF16)
    for h in range(total.shape[0] // HEAD_WIDTH):
        part = slice(h * HEAD_WIDTH, (h + 1) * HEAD_WIDTH)
        rows_ref[:, part] = total[part].T.astype(BF16)


def project_kernel(at_ref, a_ref, w_ref, *refs):
    *out_refs, held, sems = refs
    for d, copy in enumerate(fetch(at_ref, w_ref, held, sems)):
        copy.wait()
        out_refs[d][...] = dot(a_ref[...], held[d]).astype(out_refs[d].dtype)


def attention_kernel(
    len_ref,
    q_ref,
    ks_ref,
    vs_ref,
    g_ref,
    da_ref,
    dat_ref,
    att_ref,
    dq_ref,
    dks_ref,
    dvs_ref,
    dg_ref,
    k_all,
    v_all,
    dk_acc,
    dv_acc,
    *,
    scale,
):
    n = len_ref[0]
    half = g_ref.shape[0] // 2
    prefix = half * g_ref.shape[1]
    suffix = ks_ref.shape[0]
    k_all[:prefix, :] = g_ref[:half].reshape(prefix, HEAD_WIDTH)
    v_all[:prefix, :] = g_ref[half:].reshape(prefix, HEAD_WIDTH)
    k_all[prefix:, :] = ks_ref[...]
    v_all[prefix:, :] = vs_ref[...]
    k_t = k_all[...].T
    v_t = v_all[...].T
    heads = q_ref.shape[1] // 128
    key_at = iota((suffix, 2 * suffix), 0)
    slot_at = iota((suffix, 2 * suffix), 1) % suffix
    hidden = jnp.logical_or(key_at > slot_at, key_at >= n)
    live = iota((1, 2 * suffix), 1) % suffix < n
    to_log2 = scale * 1.4426950408889634
    for pair in range(heads // 2):
        one = slice(pair * 256, pair * 256 + 128)
        two = slice(pair * 256 + 128, pair * 256 + 256)
        q2 = jnp.concatenate([q_ref[:, one], q_ref[:, two]], axis=0)
        da2 = jnp.concatenate([da_ref[:, one], da_ref[:, two]], axis=0)
        dat2 = jnp.concatenate([dat_ref[one, :], dat_ref[two, :]], axis=1)
        s_pre = dot_nt(k_all[:prefix], q2)
        s_suf = jnp.where(hidden, -jnp.inf, dot_nt(k_all[prefix:], q2))
        peak = jnp.maximum(
            jnp.max(s_pre, axis=0, keepdims=True), jnp.max(s_suf, axis=0, keepdims=True)
        )
        w = jnp.concatenate(
            [jnp.exp2((s_pre - peak) * to_log2), jnp.exp2((s_suf - peak) * to_log2)], axis=0
        )
        inverse = 1.0 / jnp.sum(w, axis=0, keepdims=True)
        out_t = dot(v_t, w.astype(BF16)) * inverse
        out_t = jnp.where(live, out_t, 0.0).astype(BF16).astype(F32)
        att_ref[:, one] = out_t[:, :128].T.astype(BF16)
        att_ref[:, two] = out_t[:, 128:].T.astype(BF16)
        dots = jnp.sum(out_t * dat2.astype(F32), axis=0, keepdims=True)
        probs = w * inverse
        ds = (probs * (dot(v_all[...], dat2) - dots)).astype(BF16)
        dq_t = dot(k_t, ds) * scale
        dq_ref[:, one] = dq_t[:, :128].T.astype(BF16)
        dq_ref[:, two] = dq_t[:, 128:].T.astype(BF16)
        dk = dot(ds, q2)
        dv = dot(probs.astype(BF16), da2)
        if pair == 0:
            dk_acc[...] = dk
            dv_acc[...] = dv
        else:
            dk_acc[...] += dk
            dv_acc[...] += dv
    dg_ref[:half] = (dk_acc[:prefix] * scale).astype(BF16).reshape(half, -1, HEAD_WIDTH)
    dg_ref[half:] = dv_acc[:prefix].astype(BF16).reshape(half, -1, HEAD_WIDTH)
    dks_ref[...] = (dk_acc[prefix:] * scale).astype(BF16)
    dvs_ref[...] = dv_acc[prefix:].astype(BF16)


def whole(memory=pltpu.VMEM):
    return pl.BlockSpec(memory_space=memory)


def params(mib=24):
    return pltpu.CompilerParams(vmem_limit_bytes=mib * 1024 * 1024)


def shape(*dims, dtype=BF16):
    return jax.ShapeDtypeStruct(dims, dtype)


def shards(
    queries,
    suffix_keys,
    suffix_values,
    prefix_keys,
    prefix_values,
    block_prompt,
    rollout_prompt,
    suffix_length,
    out_weight,
    out_grad,
):
    homes = lax.axis_size("seq")
    cuts = lax.axis_size("tensor")
    rows, width = queries.shape
    features = out_grad.shape[1]
    per_prompt = homes // PROMPTS
    prefix_rows = prefix_keys.shape[0]
    served = 2 * prefix_rows // SERVERS
    tall = SERVERS * (served + 2)
    span = per_prompt * served
    groups = [[g + i for i in range(SERVERS)] for g in range(0, homes, SERVERS)]
    at = lax.axis_index("tensor").astype(jnp.int32).reshape(1)

    def swap(x):
        return lax.all_to_all(x, "seq", 0, 0, tiled=True, axis_index_groups=groups)

    turn = lambda x, d: lax.ppermute(x, "tensor", [(i, (i + d) % cuts) for i in range(cuts)])
    grads = [out_grad] + [turn(out_grad, cuts - d) for d in range(1, cuts)]
    turns = homes // SERVERS
    own = (lax.axis_index("seq") // SERVERS).astype(jnp.int32).reshape(1)
    sent = pl.pallas_call(
        functools.partial(pack_kernel, rows=served, turns=turns),
        out_shape=shape(turns * tall, HEAD_WIDTH),
        in_specs=[whole(pltpu.SMEM)] * 2 + [whole()] * 2,
        out_specs=whole(),
        compiler_params=params(),
        name="pack",
    )(block_prompt, rollout_prompt, prefix_keys, prefix_values)
    pieces = lax.all_to_all(
        sent.reshape(homes, served // 2 + 1, 2, HEAD_WIDTH), "seq", 0, 0, tiled=True
    ).reshape(turns * tall, HEAD_WIDTH)
    pieces, grads = lax.optimization_barrier((pieces, grads))
    picked, meta = pl.pallas_call(
        functools.partial(
            select_kernel, per_prompt=per_prompt, servers=SERVERS, rows=served, turns=turns
        ),
        out_shape=(shape(SERVERS, span, HEAD_WIDTH), shape(homes, 128)),
        in_specs=[whole(pltpu.SMEM), whole()],
        out_specs=(whole(), whole()),
        compiler_params=params(),
        name="select",
    )(own, pieces)
    gathered = swap(picked)
    home_map = pl.pallas_call(
        functools.partial(map_kernel, per_prompt=per_prompt, servers=SERVERS),
        out_shape=shape(2 * homes, 2 * per_prompt * SERVERS),
        in_specs=[whole(pltpu.SMEM), whole()],
        out_specs=whole(),
        compiler_params=params(),
        name="home_map",
    )(own, meta)

    weight = whole(pltpu.HBM)
    held = [
        pltpu.VMEM((cuts, width, features), BF16),
        pltpu.SemaphoreType.DMA((cuts,)),
    ]
    d_rows, d_cols = pl.pallas_call(
        grad_rows_kernel,
        out_shape=(shape(rows, width), shape(width, rows)),
        in_specs=[whole(pltpu.SMEM)] * 2 + [whole()] * cuts + [weight],
        out_specs=(whole(), whole()),
        scratch_shapes=held,
        compiler_params=params(),
        name="grad_rows",
    )(at, suffix_length, *grads, pltpu.with_memory_space_constraint(out_weight, pltpu.HBM))

    keys = prefix_keys.shape[0] * per_prompt + rows
    attended, d_queries, d_suffix_keys, d_suffix_values, d_gathered = pl.pallas_call(
        functools.partial(attention_kernel, scale=HEAD_WIDTH**-0.5),
        out_shape=(
            shape(rows, width),
            shape(rows, width),
            shape(rows, HEAD_WIDTH),
            shape(rows, HEAD_WIDTH),
            shape(SERVERS, span, HEAD_WIDTH),
        ),
        in_specs=[whole(pltpu.SMEM)] + [whole()] * 6,
        out_specs=(whole(),) * 5,
        scratch_shapes=[
            pltpu.VMEM((keys, HEAD_WIDTH), BF16),
            pltpu.VMEM((keys, HEAD_WIDTH), BF16),
            pltpu.VMEM((keys, HEAD_WIDTH), F32),
            pltpu.VMEM((keys, HEAD_WIDTH), F32),
        ],
        compiler_params=params(),
        name="attention",
    )(suffix_length, queries, suffix_keys, suffix_values, gathered, d_rows, d_cols)

    head_terms = pl.pallas_call(
        project_kernel,
        out_shape=(shape(rows, features, dtype=F32),) + (shape(rows, features),) * (cuts - 1),
        in_specs=[whole(pltpu.SMEM), whole(), weight],
        out_specs=(whole(),) * cuts,
        scratch_shapes=held,
        compiler_params=params(),
        name="project",
    )(at, attended, pltpu.with_memory_space_constraint(out_weight, pltpu.HBM))
    projected = head_terms[0]
    for d in range(1, cuts):
        projected = projected + turn(head_terms[d], d).astype(F32)

    sums = pl.pallas_call(
        functools.partial(combine_kernel, turns=turns),
        out_shape=shape(homes * served, HEAD_WIDTH),
        in_specs=[whole(), whole()],
        out_specs=whole(),
        compiler_params=params(),
        name="combine",
    )(home_map, swap(d_gathered))
    back = lax.all_to_all(
        sums.reshape(homes, served, HEAD_WIDTH), "seq", 0, 0, tiled=True
    ).reshape(turns, 2 * prefix_rows, HEAD_WIDTH)
    d_prefix_keys, d_prefix_values = pl.pallas_call(
        home_sum_kernel,
        out_shape=(shape(prefix_rows, HEAD_WIDTH),) * 2,
        in_specs=[whole()],
        out_specs=(whole(), whole()),
        compiler_params=params(),
        name="home_sum",
    )(back)
    return (
        projected.astype(BF16),
        d_queries,
        d_suffix_keys,
        d_suffix_values,
        d_prefix_keys,
        d_prefix_values,
    )


def solution(mesh):
    split = P("seq", "tensor")
    in_specs = (split,) * 5 + (P("seq"),) * 3 + (P("tensor", None), split)
    return jax.shard_map(
        shards, mesh=mesh, in_specs=in_specs, out_specs=(split,) * 6, check_vma=False
    )
```

```python
import functools

import jax
import jax.numpy as jnp
from jax import lax
from jax.experimental import pallas as pl
from jax.experimental.pallas import tpu as pltpu
from jax.sharding import PartitionSpec as P

HEAD_WIDTH = 128
PROMPTS = 8
SERVERS = 16
F32 = jnp.float32
BF16 = jnp.bfloat16
NT = (((1,), (1,)), ((), ()))


def dot(a, b):
    return jnp.dot(a, b, preferred_element_type=F32)


def dot_nt(a, b):
    return lax.dot_general(a, b, NT, preferred_element_type=F32)


def iota(shape, dim):
    return lax.broadcasted_iota(jnp.int32, shape, dim)


def one_hot(left, right):
    return (left == right).astype(BF16)


def fiota(shape, dim):
    return iota(shape, dim).astype(F32)


def pack_kernel(
    block_ref, rollout_ref, keys_hbm, values_hbm, sent_ref, keys_ref, values_ref, sems, *, rows, turns
):
    copies = [
        pltpu.make_async_copy(keys_hbm, keys_ref, sems.at[0]),
        pltpu.make_async_copy(values_hbm, values_ref, sems.at[1]),
    ]
    for copy in copies:
        copy.start()
    total, tall = keys_ref.shape[0], sent_ref.shape[0] // turns
    group = rows + 2
    row, col = iota((tall, total), 0), iota((tall, total), 1)
    place = row % group
    source = jnp.where(place < rows, (row // group) * rows + place, -1)
    take_keys, take_values = one_hot(source, col), one_hot(source - total, col)
    for copy in copies:
        copy.wait()
    packed = dot(take_keys, keys_ref[...])
    packed = packed + dot(take_values, values_ref[...])
    row, lane = iota(packed.shape, 0), iota(packed.shape, 1)
    names = jnp.where(lane == 0, block_ref[0], jnp.where(lane == 1, rollout_ref[0], 0))
    packed = jnp.where(row % group >= rows, names.astype(F32), packed).astype(BF16)
    for g in range(turns):
        sent_ref[g * tall : (g + 1) * tall, :] = packed


def swap_pairs(tall, outer):
    row, col = iota((tall, tall), 0), iota((tall, tall), 1)
    pair = row // 2
    return one_hot((pair % outer * (tall // 2 // outer) + pair // outer) * 2 + row % 2, col)


def block_codes(meta, own, *, per_prompt, servers):
    blocks = meta.shape[0]
    block_prompt = meta[:, 0:1].astype(F32)
    named = one_hot(block_prompt, fiota((blocks, 128), 1))
    same = dot_nt(named, named)
    row, col = iota((blocks, blocks), 0), iota((blocks, blocks), 1)
    rank = jnp.sum(jnp.where(col < row, same, 0.0), axis=1, keepdims=True)
    take = one_hot(iota((servers, blocks), 0) + own * servers, iota((servers, blocks), 1))
    return block_prompt * per_prompt + rank, dot(take, meta)[:, 1:2]


def select_kernel(own_ref, pieces_ref, picked_ref, meta_ref, *, per_prompt, servers, rows, turns):
    tall = servers * (rows + 2)
    swap = swap_pairs(tall, servers)
    pieces = [
        dot(swap, pieces_ref[g * tall : (g + 1) * tall]).astype(BF16) for g in range(turns)
    ]
    each, blocks = 2 * servers, servers * turns
    meta = jnp.concatenate([p[rows // 2 * each :] for p in pieces])
    one_each = one_hot(iota((blocks, 2 * blocks), 0) * 2, iota((blocks, 2 * blocks), 1))
    meta = dot(one_each, meta).astype(BF16)
    meta_ref[...] = meta
    code, rollout = block_codes(meta, own_ref[0], per_prompt=per_prompt, servers=servers)
    span, wants = 2 * per_prompt, 2 * per_prompt * servers
    spread = iota((blocks, 2 * blocks), 1) // 2 == iota((blocks, 2 * blocks), 0)
    have = jnp.sum(jnp.where(spread, code, 0.0), axis=0, keepdims=True) * 2
    have = have + (iota((1, 2 * blocks), 1) % 2).astype(F32)
    want = jnp.broadcast_to(rollout.reshape(servers, 1, 1), (servers, span, 1))
    want = want.reshape(wants, 1) * span + (iota((wants, 1), 0) % span).astype(F32)
    choose = one_hot(want, have)
    for p in range(rows // 2):
        from_all = jnp.concatenate([part[p * each : (p + 1) * each] for part in pieces])
        picked = dot(choose, from_all).astype(BF16)
        picked_ref[:, p * span : (p + 1) * span, :] = picked.reshape(servers, span, HEAD_WIDTH)


def map_kernel(own_ref, meta_ref, map_ref, *, per_prompt, servers):
    code, rollout = block_codes(
        meta_ref[...], own_ref[0], per_prompt=per_prompt, servers=servers
    )
    blocks = code.shape[0]
    tall, wants = map_ref.shape
    span = 2 * per_prompt
    eye = iota((blocks, blocks), 0) == iota((blocks, blocks), 1)
    code_row = jnp.sum(jnp.where(eye, code, 0.0), axis=0, keepdims=True)
    mine = iota((tall, blocks), 0) // 2 == iota((tall, blocks), 1)
    have = jnp.sum(jnp.where(mine, code_row, 0.0), axis=1, keepdims=True) * 2
    have = have + (iota((tall, 1), 0) % 2).astype(F32)
    spread = iota((servers, wants), 1) // span == iota((servers, wants), 0)
    want = jnp.sum(jnp.where(spread, rollout, 0.0), axis=0, keepdims=True) * span
    want = want + (iota((1, wants), 1) % span).astype(F32)
    map_ref[...] = one_hot(have, want)


def combine_kernel(map_ref, terms_ref, out_ref, *, turns):
    servers, tall, _ = terms_ref.shape
    wants = map_ref.shape[1]
    span, each = wants // servers, map_ref.shape[0] // turns
    sums = []
    for p in range(tall // span):
        terms = terms_ref[:, p * span : (p + 1) * span, :].reshape(wants, HEAD_WIDTH)
        sums.append(dot(map_ref[...], terms).astype(BF16))
    rows = each * len(sums)
    swap = swap_pairs(rows, len(sums))
    for g in range(turns):
        part = jnp.concatenate([s[g * each : (g + 1) * each] for s in sums])
        out_ref[g * rows : (g + 1) * rows, :] = dot(swap, part).astype(BF16)


def home_sum_kernel(terms_ref, keys_ref, values_ref):
    total = jnp.sum(terms_ref[...].astype(F32), axis=0)
    half = keys_ref.shape[0]
    keys_ref[...] = total[:half].astype(BF16)
    values_ref[...] = total[half:].astype(BF16)


def fetch(at_ref, w_ref, held, sems, turns, cuts):
    width = held.shape[2]
    copies = []
    for i, d in enumerate(turns):
        start = pl.multiple_of(lax.rem(at_ref[0] + d, cuts) * width, width)
        copies.append(
            pltpu.make_async_copy(w_ref.at[:, pl.ds(start, width)], held.at[i], sems.at[i])
        )
        copies[i].start()
    return copies


def grad_rows_kernel(at_ref, *refs, turns, cuts):
    *g_refs, w_ref, total_ref, held, sems = refs
    total = None
    for i, copy in enumerate(fetch(at_ref, w_ref, held, sems, turns, cuts)):
        copy.wait()
        term = dot_nt(held[i], g_refs[i][...])
        total = term if total is None else total + term
    total_ref[...] = total


def grad_rows_end_kernel(
    at_ref, len_ref, first_ref, g_ref, w_ref, rows_ref, cols_ref, held, sems, *, turns, cuts
):
    (copy,) = fetch(at_ref, w_ref, held, sems, turns, cuts)
    copy.wait()
    total = first_ref[...] + dot_nt(held[0], g_ref[...])
    live = iota(total.shape, 1) < len_ref[0]
    total = jnp.where(live, total, 0.0)
    cols_ref[...] = total.astype(BF16)
    for h in range(total.shape[0] // HEAD_WIDTH):
        part = slice(h * HEAD_WIDTH, (h + 1) * HEAD_WIDTH)
        rows_ref[:, part] = total[part].T.astype(BF16)


def project_kernel(at_ref, a_ref, w_ref, *refs, turns, cuts):
    *out_refs, held, sems = refs
    for i, copy in enumerate(fetch(at_ref, w_ref, held, sems, turns, cuts)):
        copy.wait()
        out_refs[i][...] = dot(a_ref[...], held[i]).astype(out_refs[i].dtype)


def attention_kernel(
    len_ref,
    q_ref,
    ks_ref,
    vs_ref,
    g_ref,
    da_ref,
    dat_ref,
    att_ref,
    dq_ref,
    dks_ref,
    dvs_ref,
    dg_ref,
    k_all,
    v_all,
    dk_acc,
    dv_acc,
    *,
    scale,
    together,
):
    n = len_ref[0]
    half = g_ref.shape[0] // 2
    prefix = half * g_ref.shape[1]
    suffix = ks_ref.shape[0]
    k_all[:prefix, :] = g_ref[:half].reshape(prefix, HEAD_WIDTH)
    v_all[:prefix, :] = g_ref[half:].reshape(prefix, HEAD_WIDTH)
    k_all[prefix:, :] = ks_ref[...]
    v_all[prefix:, :] = vs_ref[...]
    k_t = k_all[...].T
    v_t = v_all[...].T
    lanes = together * suffix
    key_at = iota((suffix, lanes), 0)
    slot_at = iota((suffix, lanes), 1) % suffix
    hidden = jnp.logical_or(key_at > slot_at, key_at >= n)
    live = iota((1, lanes), 1) % suffix < n
    to_log2 = scale * 1.4426950408889634
    steps = q_ref.shape[1] // (together * HEAD_WIDTH)

    def heads(step):
        first = step * together
        return [slice((first + i) * HEAD_WIDTH, (first + i + 1) * HEAD_WIDTH) for i in range(together)]

    def rows_of(ref, step):
        return jnp.concatenate([ref[:, h] for h in heads(step)], axis=0)

    def put_rows(ref, step, x):
        for i, h in enumerate(heads(step)):
            ref[:, h] = x[:, i * suffix : (i + 1) * suffix].T.astype(BF16)

    def scores(step):
        s = dot_nt(k_all[...], rows_of(q_ref, step))
        return s[:prefix], jnp.where(hidden, -jnp.inf, s[prefix:])

    def softmax(s):
        peak = jnp.maximum(*[jnp.max(part, axis=0, keepdims=True) for part in s])
        parts = [jnp.exp2((part - peak) * to_log2) for part in s]
        total = sum(jnp.sum(part, axis=0, keepdims=True) for part in parts)
        w = jnp.concatenate(parts, axis=0)
        return w, w.astype(BF16), 1.0 / total

    ready = softmax(scores(0))
    for step in range(steps):
        last = step + 1 == steps
        if not last:
            coming = scores(step + 1)
        w, w_rounded, inverse = ready
        out_t = dot(v_t, w_rounded) * inverse
        out_t = jnp.where(live, out_t, 0.0).astype(BF16).astype(F32)
        put_rows(att_ref, step, out_t)
        dat = jnp.concatenate([dat_ref[h, :] for h in heads(step)], axis=1)
        dots = jnp.sum(out_t * dat.astype(F32), axis=0, keepdims=True)
        if not last:
            ready = softmax(coming)
        probs = w * inverse
        ds = (probs * (dot(v_all[...], dat) - dots)).astype(BF16)
        put_rows(dq_ref, step, dot(k_t, ds) * scale)
        dk = dot(ds, rows_of(q_ref, step))
        dv = dot(probs.astype(BF16), rows_of(da_ref, step))
        if step == 0:
            dk_acc[...] = dk
            dv_acc[...] = dv
        else:
            dk_acc[...] += dk
            dv_acc[...] += dv
    dg_ref[:half] = (dk_acc[:prefix] * scale).astype(BF16).reshape(half, -1, HEAD_WIDTH)
    dg_ref[half:] = dv_acc[:prefix].astype(BF16).reshape(half, -1, HEAD_WIDTH)
    dks_ref[...] = (dk_acc[prefix:] * scale).astype(BF16)
    dvs_ref[...] = dv_acc[prefix:].astype(BF16)


def in_hbm(x):
    return pltpu.with_memory_space_constraint(x, pltpu.HBM)


def whole(memory=pltpu.VMEM):
    return pl.BlockSpec(memory_space=memory)


def params(mib=24):
    return pltpu.CompilerParams(vmem_limit_bytes=mib * 1024 * 1024)


def shape(*dims, dtype=BF16):
    return jax.ShapeDtypeStruct(dims, dtype)


def shards(
    queries,
    suffix_keys,
    suffix_values,
    prefix_keys,
    prefix_values,
    block_prompt,
    rollout_prompt,
    suffix_length,
    out_weight,
    out_grad,
):
    homes = lax.axis_size("seq")
    cuts = lax.axis_size("tensor")
    rows, width = queries.shape
    features = out_grad.shape[1]
    per_prompt = homes // PROMPTS
    prefix_rows = prefix_keys.shape[0]
    served = 2 * prefix_rows // SERVERS
    tall = SERVERS * (served + 2)
    span = per_prompt * served
    groups = [[g + i for i in range(SERVERS)] for g in range(0, homes, SERVERS)]
    at = lax.axis_index("tensor").astype(jnp.int32).reshape(1)

    def swap(x):
        return lax.all_to_all(x, "seq", 0, 0, tiled=True, axis_index_groups=groups)

    turn = lambda x, d: lax.ppermute(x, "tensor", [(i, (i + d) % cuts) for i in range(cuts)])
    grads = [out_grad] + [turn(out_grad, cuts - d) for d in range(1, cuts)]
    turns = homes // SERVERS
    own = (lax.axis_index("seq") // SERVERS).astype(jnp.int32).reshape(1)
    sent = pl.pallas_call(
        functools.partial(pack_kernel, rows=served, turns=turns),
        out_shape=shape(turns * tall, HEAD_WIDTH),
        in_specs=[whole(pltpu.SMEM)] * 2 + [whole(pltpu.HBM)] * 2,
        out_specs=whole(),
        scratch_shapes=[
            pltpu.VMEM(prefix_keys.shape, BF16),
            pltpu.VMEM(prefix_keys.shape, BF16),
            pltpu.SemaphoreType.DMA((2,)),
        ],
        compiler_params=params(),
        name="pack",
    )(block_prompt, rollout_prompt, in_hbm(prefix_keys), in_hbm(prefix_values))
    pieces = lax.all_to_all(
        sent.reshape(homes, served // 2 + 1, 2, HEAD_WIDTH), "seq", 0, 0, tiled=True
    ).reshape(turns * tall, HEAD_WIDTH)
    pieces, grads[1], grads[-1] = lax.optimization_barrier((pieces, grads[1], grads[-1]))
    picked, meta = pl.pallas_call(
        functools.partial(
            select_kernel, per_prompt=per_prompt, servers=SERVERS, rows=served, turns=turns
        ),
        out_shape=(shape(SERVERS, span, HEAD_WIDTH), shape(homes, 128)),
        in_specs=[whole(pltpu.SMEM), whole()],
        out_specs=(whole(), whole()),
        compiler_params=params(),
        name="select",
    )(own, pieces)
    gathered = swap(picked)
    home_map = pl.pallas_call(
        functools.partial(map_kernel, per_prompt=per_prompt, servers=SERVERS),
        out_shape=shape(2 * homes, 2 * per_prompt * SERVERS),
        in_specs=[whole(pltpu.SMEM), whole()],
        out_specs=whole(),
        compiler_params=params(),
        name="home_map",
    )(own, meta)

    weight = whole(pltpu.HBM)
    out_weight = in_hbm(out_weight)

    def held(turns):
        return [
            pltpu.VMEM((len(turns), width, features), BF16),
            pltpu.SemaphoreType.DMA((len(turns),)),
        ]

    near = tuple(d for d in range(cuts) if d != cuts // 2)
    far = (cuts // 2,)
    first = pl.pallas_call(
        functools.partial(grad_rows_kernel, turns=near, cuts=cuts),
        out_shape=shape(width, rows, dtype=F32),
        in_specs=[whole(pltpu.SMEM)] + [whole()] * len(near) + [weight],
        out_specs=whole(),
        scratch_shapes=held(near),
        compiler_params=params(),
        name="grad_rows",
    )(at, *[grads[d] for d in near], out_weight)
    d_rows, d_cols = pl.pallas_call(
        functools.partial(grad_rows_end_kernel, turns=far, cuts=cuts),
        out_shape=(shape(rows, width), shape(width, rows)),
        in_specs=[whole(pltpu.SMEM)] * 2 + [whole()] * 2 + [weight],
        out_specs=(whole(), whole()),
        scratch_shapes=held(far),
        compiler_params=params(),
        name="grad_rows_end",
    )(at, suffix_length, first, grads[cuts // 2], out_weight)

    gathered, home_map = lax.optimization_barrier((gathered, home_map))
    keys = prefix_keys.shape[0] * per_prompt + rows
    attended, d_queries, d_suffix_keys, d_suffix_values, d_gathered = pl.pallas_call(
        functools.partial(attention_kernel, scale=HEAD_WIDTH**-0.5, together=4),
        out_shape=(
            shape(rows, width),
            shape(rows, width),
            shape(rows, HEAD_WIDTH),
            shape(rows, HEAD_WIDTH),
            shape(SERVERS, span, HEAD_WIDTH),
        ),
        in_specs=[whole(pltpu.SMEM)] + [whole()] * 6,
        out_specs=(whole(),) * 5,
        scratch_shapes=[
            pltpu.VMEM((keys, HEAD_WIDTH), BF16),
            pltpu.VMEM((keys, HEAD_WIDTH), BF16),
            pltpu.VMEM((keys, HEAD_WIDTH), F32),
            pltpu.VMEM((keys, HEAD_WIDTH), F32),
        ],
        compiler_params=params(),
        name="attention",
    )(suffix_length, queries, suffix_keys, suffix_values, gathered, d_rows, d_cols)

    def project(turns, own):
        return pl.pallas_call(
            functools.partial(project_kernel, turns=turns, cuts=cuts),
            out_shape=[shape(rows, features, dtype=F32 if d == own else BF16) for d in turns],
            in_specs=[whole(pltpu.SMEM), whole(), weight],
            out_specs=[whole()] * len(turns),
            scratch_shapes=held(turns),
            compiler_params=params(),
            name="project",
        )(at, attended, out_weight)

    one_hop = [d for d in near if d > 0]
    terms_near = project(one_hop, 0)
    terms_far = project((cuts // 2, 0), 0)
    arrived = [turn(term, d) for d, term in zip(one_hop, terms_near)]
    projected = terms_far[1] + sum(x.astype(F32) for x in arrived)
    projected = projected + turn(terms_far[0], cuts // 2).astype(F32)

    terms, _ = lax.optimization_barrier((swap(d_gathered), (arrived, terms_far)))
    sums = pl.pallas_call(
        functools.partial(combine_kernel, turns=turns),
        out_shape=shape(homes * served, HEAD_WIDTH),
        in_specs=[whole(), whole()],
        out_specs=whole(),
        compiler_params=params(),
        name="combine",
    )(home_map, terms)
    back = lax.all_to_all(
        sums.reshape(homes, served, HEAD_WIDTH), "seq", 0, 0, tiled=True
    ).reshape(turns, 2 * prefix_rows, HEAD_WIDTH)
    d_prefix_keys, d_prefix_values = pl.pallas_call(
        home_sum_kernel,
        out_shape=(shape(prefix_rows, HEAD_WIDTH),) * 2,
        in_specs=[whole()],
        out_specs=(whole(), whole()),
        compiler_params=params(),
        name="home_sum",
    )(back)
    return (
        projected.astype(BF16),
        d_queries,
        d_suffix_keys,
        d_suffix_values,
        d_prefix_keys,
        d_prefix_values,
    )


def solution(mesh):
    split = P("seq", "tensor")
    in_specs = (split,) * 5 + (P("seq"),) * 3 + (P("tensor", None), split)
    return jax.shard_map(
        shards, mesh=mesh, in_specs=in_specs, out_specs=(split,) * 6, check_vma=False
    )
```

```python
import functools

import jax
import jax.numpy as jnp
import numpy as np
from jax import lax
from jax.experimental import pallas as pl
from jax.experimental.pallas import tpu as pltpu
from jax.sharding import PartitionSpec as P

HEAD_WIDTH = 128
PROMPTS = 8
SERVERS = 16
F32 = jnp.float32
BF16 = jnp.bfloat16
NT = (((1,), (1,)), ((), ()))


def dot(a, b):
    return jnp.dot(a, b, preferred_element_type=F32)


def dot_nt(a, b):
    return lax.dot_general(a, b, NT, preferred_element_type=F32)


def iota(shape, dim):
    return lax.broadcasted_iota(jnp.int32, shape, dim)


def one_hot(left, right):
    return (left == right).astype(BF16)


def fiota(shape, dim):
    return iota(shape, dim).astype(F32)


def pack_kernel(
    block_ref, rollout_ref, keys_hbm, values_hbm, sent_ref, keys_ref, values_ref, sems, *, rows, turns
):
    copies = [
        pltpu.make_async_copy(keys_hbm, keys_ref, sems.at[0]),
        pltpu.make_async_copy(values_hbm, values_ref, sems.at[1]),
    ]
    for copy in copies:
        copy.start()
    total, tall = keys_ref.shape[0], sent_ref.shape[0] // turns
    group = rows + 2
    row, col = iota((tall, total), 0), iota((tall, total), 1)
    place = row % group
    source = jnp.where(place < rows, (row // group) * rows + place, -1)
    take_keys, take_values = one_hot(source, col), one_hot(source - total, col)
    for copy in copies:
        copy.wait()
    packed = dot(take_keys, keys_ref[...])
    packed = packed + dot(take_values, values_ref[...])
    row, lane = iota(packed.shape, 0), iota(packed.shape, 1)
    names = jnp.where(lane == 0, block_ref[0], jnp.where(lane == 1, rollout_ref[0], 0))
    packed = jnp.where(row % group >= rows, names.astype(F32), packed).astype(BF16)
    for g in range(turns):
        sent_ref[g * tall : (g + 1) * tall, :] = packed


def swap_pairs(tall, outer):
    rows = np.arange(tall).reshape(outer, -1, 2).swapaxes(0, 1).reshape(tall)
    return jnp.asarray(np.eye(tall)[rows], BF16)


def name_rows(blocks, group):
    take = np.zeros((blocks, blocks, group))
    take[np.arange(blocks), np.arange(blocks), group - 2] = 1
    return jnp.asarray(take.reshape(blocks, blocks * group), BF16)


def block_codes(meta, *, per_prompt):
    blocks = meta.shape[0]
    first_lane = one_hot(iota((8, 128), 1), 0)
    prompt_row = dot_nt(first_lane, meta)[0:1]
    same = meta[:, 0:1].astype(F32) == prompt_row
    before = iota((blocks, blocks), 0) < iota((blocks, blocks), 1)
    rank = jnp.sum(jnp.where(jnp.logical_and(same, before), 1.0, 0.0), axis=0, keepdims=True)
    return prompt_row * per_prompt + rank


def own_rollouts(meta, own, *, servers, span):
    wants, blocks = servers * span, meta.shape[0]
    take = one_hot(iota((wants, blocks), 0) // span + own * servers, iota((wants, blocks), 1))
    return dot(take, meta)[:, 1:2]


def select_kernel(
    own_ref,
    pieces_ref,
    swap_ref,
    take_ref,
    picked_ref,
    meta_ref,
    *,
    per_prompt,
    servers,
    rows,
    turns,
):
    tall, blocks = servers * (rows + 2), servers * turns
    each, span = 2 * servers, 2 * per_prompt
    wants = span * servers
    meta = dot(take_ref[...], pieces_ref[...]).astype(BF16)
    meta_ref[...] = meta
    swap = swap_ref[...]
    pieces = [
        dot(swap, pieces_ref[g * tall : (g + 1) * tall]).astype(BF16) for g in range(turns)
    ]
    code = jnp.broadcast_to(block_codes(meta, per_prompt=per_prompt), (8, blocks))
    spread = one_hot(iota((blocks, 2 * blocks), 1) // 2, iota((blocks, 2 * blocks), 0))
    have = dot(code.astype(BF16), spread)[0:1] * 2
    have = have + (iota((1, 2 * blocks), 1) % 2).astype(F32)
    want = own_rollouts(meta, own_ref[0], servers=servers, span=span) * span
    want = want + (iota((wants, 1), 0) % span).astype(F32)
    choose = one_hot(want, have)
    for p in range(rows // 2):
        from_all = jnp.concatenate([part[p * each : (p + 1) * each] for part in pieces])
        picked = dot(choose, from_all).astype(BF16)
        picked_ref[:, p * span : (p + 1) * span, :] = picked.reshape(servers, span, HEAD_WIDTH)


def map_kernel(own_ref, meta_ref, map_ref, *, per_prompt, servers):
    meta = meta_ref[...]
    blocks = meta.shape[0]
    tall, wants = map_ref.shape
    span = 2 * per_prompt
    code_row = block_codes(meta, per_prompt=per_prompt)
    mine = iota((tall, blocks), 0) // 2 == iota((tall, blocks), 1)
    have = jnp.sum(jnp.where(mine, code_row, 0.0), axis=1, keepdims=True) * 2
    have = have + (iota((tall, 1), 0) % 2).astype(F32)
    rollout = own_rollouts(meta, own_ref[0], servers=servers, span=1)
    spread = iota((servers, wants), 1) // span == iota((servers, wants), 0)
    want = jnp.sum(jnp.where(spread, rollout, 0.0), axis=0, keepdims=True) * span
    want = want + (iota((1, wants), 1) % span).astype(F32)
    map_ref[...] = one_hot(have, want)


def combine_kernel(map_ref, terms_ref, swap_ref, out_ref, *, turns):
    servers, tall, _ = terms_ref.shape
    wants = map_ref.shape[1]
    span, each = wants // servers, map_ref.shape[0] // turns
    sums = []
    for p in range(tall // span):
        terms = terms_ref[:, p * span : (p + 1) * span, :].reshape(wants, HEAD_WIDTH)
        sums.append(dot(map_ref[...], terms).astype(BF16))
    rows = each * len(sums)
    swap = swap_ref[...]
    for g in range(turns):
        part = jnp.concatenate([s[g * each : (g + 1) * each] for s in sums])
        out_ref[g * rows : (g + 1) * rows, :] = dot(swap, part).astype(BF16)


def home_sum_kernel(terms_ref, keys_ref, values_ref):
    total = jnp.sum(terms_ref[...].astype(F32), axis=0)
    half = keys_ref.shape[0]
    keys_ref[...] = total[:half].astype(BF16)
    values_ref[...] = total[half:].astype(BF16)


def fetch(at_ref, w_ref, held, sems, turns, cuts):
    width = held.shape[2]
    copies = []
    for i, d in enumerate(turns):
        start = pl.multiple_of(lax.rem(at_ref[0] + d, cuts) * width, width)
        copies.append(
            pltpu.make_async_copy(w_ref.at[:, pl.ds(start, width)], held.at[i], sems.at[i])
        )
        copies[i].start()
    return copies


def grad_rows_kernel(at_ref, *refs, turns, cuts):
    *in_refs, w_ref, total_ref, held, sems = refs
    copies = fetch(at_ref, w_ref, held, sems, turns, cuts)
    total = in_refs[-1][...] if len(in_refs) > len(turns) else None
    for i, copy in enumerate(copies):
        copy.wait()
        term = dot_nt(held[i], in_refs[i][...])
        total = term if total is None else total + term
    total_ref[...] = total


def grad_rows_end_kernel(
    at_ref, len_ref, first_ref, g_ref, w_ref, rows_ref, cols_ref, held, sems, *, turns, cuts
):
    (copy,) = fetch(at_ref, w_ref, held, sems, turns, cuts)
    copy.wait()
    total = first_ref[...] + dot_nt(held[0], g_ref[...])
    live = iota(total.shape, 1) < len_ref[0]
    total = jnp.where(live, total, 0.0)
    cols_ref[...] = total.astype(BF16)
    for h in range(total.shape[0] // HEAD_WIDTH):
        part = slice(h * HEAD_WIDTH, (h + 1) * HEAD_WIDTH)
        rows_ref[:, part] = total[part].T.astype(BF16)


def project_kernel(at_ref, a_ref, w_ref, *refs, turns, cuts):
    *out_refs, held, sems = refs
    for i, copy in enumerate(fetch(at_ref, w_ref, held, sems, turns, cuts)):
        copy.wait()
        out_refs[i][...] = dot(a_ref[...], held[i]).astype(out_refs[i].dtype)


def attention_kernel(
    len_ref,
    q_ref,
    ks_ref,
    vs_ref,
    g_ref,
    da_ref,
    dat_ref,
    att_ref,
    dq_ref,
    dks_ref,
    dvs_ref,
    dg_ref,
    k_all,
    v_all,
    dk_acc,
    dv_acc,
    *,
    scale,
    together,
):
    n = len_ref[0]
    half = g_ref.shape[0] // 2
    prefix = half * g_ref.shape[1]
    suffix = ks_ref.shape[0]
    k_all[:prefix, :] = g_ref[:half].reshape(prefix, HEAD_WIDTH)
    v_all[:prefix, :] = g_ref[half:].reshape(prefix, HEAD_WIDTH)
    k_all[prefix:, :] = ks_ref[...]
    v_all[prefix:, :] = vs_ref[...]
    k_t = k_all[...].T
    v_t = v_all[...].T
    lanes = together * suffix
    key_at = iota((suffix, lanes), 0)
    slot_at = iota((suffix, lanes), 1) % suffix
    hidden = jnp.logical_or(key_at > slot_at, key_at >= n)
    live = iota((1, lanes), 1) % suffix < n
    to_log2 = scale * 1.4426950408889634
    steps = q_ref.shape[1] // (together * HEAD_WIDTH)

    def heads(step):
        first = step * together
        return [slice((first + i) * HEAD_WIDTH, (first + i + 1) * HEAD_WIDTH) for i in range(together)]

    def rows_of(ref, step):
        return jnp.concatenate([ref[:, h] for h in heads(step)], axis=0)

    def put_rows(ref, step, x):
        for i, h in enumerate(heads(step)):
            ref[:, h] = x[:, i * suffix : (i + 1) * suffix].T.astype(BF16)

    def scores(step):
        s = dot_nt(k_all[...], rows_of(q_ref, step))
        return s[:prefix], jnp.where(hidden, -jnp.inf, s[prefix:])

    def softmax(s):
        peak = jnp.maximum(*[jnp.max(part, axis=0, keepdims=True) for part in s])
        parts = [jnp.exp2((part - peak) * to_log2) for part in s]
        total = sum(jnp.sum(part, axis=0, keepdims=True) for part in parts)
        w = jnp.concatenate(parts, axis=0)
        return w, w.astype(BF16), 1.0 / total

    ready = softmax(scores(0))
    for step in range(steps):
        last = step + 1 == steps
        if not last:
            coming = scores(step + 1)
        w, w_rounded, inverse = ready
        out_t = dot(v_t, w_rounded) * inverse
        out_t = jnp.where(live, out_t, 0.0).astype(BF16).astype(F32)
        put_rows(att_ref, step, out_t)
        dat = jnp.concatenate([dat_ref[h, :] for h in heads(step)], axis=1)
        dots = jnp.sum(out_t * dat.astype(F32), axis=0, keepdims=True)
        if not last:
            ready = softmax(coming)
        probs = w * inverse
        dv = dot(probs.astype(BF16), rows_of(da_ref, step))
        ds = (probs * (dot(v_all[...], dat) - dots)).astype(BF16)
        put_rows(dq_ref, step, dot(k_t, ds) * scale)
        dk = dot(ds, rows_of(q_ref, step))
        if step == 0:
            dk_acc[...] = dk
            dv_acc[...] = dv
        else:
            dk_acc[...] += dk
            dv_acc[...] += dv
    dg_ref[:half] = (dk_acc[:prefix] * scale).astype(BF16).reshape(half, -1, HEAD_WIDTH)
    dg_ref[half:] = dv_acc[:prefix].astype(BF16).reshape(half, -1, HEAD_WIDTH)
    dks_ref[...] = (dk_acc[prefix:] * scale).astype(BF16)
    dvs_ref[...] = dv_acc[prefix:].astype(BF16)


def in_hbm(x):
    return pltpu.with_memory_space_constraint(x, pltpu.HBM)


def whole(memory=pltpu.VMEM):
    return pl.BlockSpec(memory_space=memory)


def params(mib=24):
    return pltpu.CompilerParams(vmem_limit_bytes=mib * 1024 * 1024)


def shape(*dims, dtype=BF16):
    return jax.ShapeDtypeStruct(dims, dtype)


def shards(
    queries,
    suffix_keys,
    suffix_values,
    prefix_keys,
    prefix_values,
    block_prompt,
    rollout_prompt,
    suffix_length,
    out_weight,
    out_grad,
):
    homes = lax.axis_size("seq")
    cuts = lax.axis_size("tensor")
    rows, width = queries.shape
    features = out_grad.shape[1]
    per_prompt = homes // PROMPTS
    prefix_rows = prefix_keys.shape[0]
    served = 2 * prefix_rows // SERVERS
    tall = SERVERS * (served + 2)
    span = per_prompt * served
    groups = [[g + i for i in range(SERVERS)] for g in range(0, homes, SERVERS)]
    at = lax.axis_index("tensor").astype(jnp.int32).reshape(1)

    def swap(x):
        return lax.all_to_all(x, "seq", 0, 0, tiled=True, axis_index_groups=groups)

    turn = lambda x, d: lax.ppermute(x, "tensor", [(i, (i + d) % cuts) for i in range(cuts)])
    grads = [out_grad] + [turn(out_grad, cuts - d) for d in range(1, cuts)]
    weight = whole(pltpu.HBM)
    out_weight = in_hbm(out_weight)

    def held(turns):
        return [
            pltpu.VMEM((len(turns), width, features), BF16),
            pltpu.SemaphoreType.DMA((len(turns),)),
        ]

    def grad_rows(turns, *before):
        return pl.pallas_call(
            functools.partial(grad_rows_kernel, turns=turns, cuts=cuts),
            out_shape=shape(width, rows, dtype=F32),
            in_specs=[whole(pltpu.SMEM)] + [whole()] * (len(turns) + len(before)) + [weight],
            out_specs=whole(),
            scratch_shapes=held(turns),
            compiler_params=params(),
            name="grad_rows",
        )(at, *[grads[d] for d in turns], *before, out_weight)

    one_hop = tuple(d for d in range(1, cuts) if d != cuts // 2)
    far = (cuts // 2,)
    first = grad_rows(one_hop, grad_rows((0,)))

    turns = homes // SERVERS
    own = (lax.axis_index("seq") // SERVERS).astype(jnp.int32).reshape(1)
    sent = pl.pallas_call(
        functools.partial(pack_kernel, rows=served, turns=turns),
        out_shape=shape(turns * tall, HEAD_WIDTH),
        in_specs=[whole(pltpu.SMEM)] * 2 + [whole(pltpu.HBM)] * 2,
        out_specs=whole(),
        scratch_shapes=[
            pltpu.VMEM(prefix_keys.shape, BF16),
            pltpu.VMEM(prefix_keys.shape, BF16),
            pltpu.SemaphoreType.DMA((2,)),
        ],
        compiler_params=params(),
        name="pack",
    )(block_prompt, rollout_prompt, in_hbm(prefix_keys), in_hbm(prefix_values))
    pieces = lax.all_to_all(
        sent.reshape(homes, served // 2 + 1, 2, HEAD_WIDTH), "seq", 0, 0, tiled=True
    ).reshape(turns * tall, HEAD_WIDTH)
    pieces, first = lax.optimization_barrier((pieces, first))
    picked, meta = pl.pallas_call(
        functools.partial(
            select_kernel, per_prompt=per_prompt, servers=SERVERS, rows=served, turns=turns
        ),
        out_shape=(shape(SERVERS, span, HEAD_WIDTH), shape(homes, 128)),
        in_specs=[whole(pltpu.SMEM)] + [whole()] * 3,
        out_specs=(whole(), whole()),
        compiler_params=params(),
        name="select",
    )(own, pieces, swap_pairs(tall, SERVERS), name_rows(homes, served + 2))
    gathered = swap(picked)
    home_map = pl.pallas_call(
        functools.partial(map_kernel, per_prompt=per_prompt, servers=SERVERS),
        out_shape=shape(2 * homes, 2 * per_prompt * SERVERS),
        in_specs=[whole(pltpu.SMEM), whole()],
        out_specs=whole(),
        compiler_params=params(),
        name="home_map",
    )(own, meta)

    d_rows, d_cols = pl.pallas_call(
        functools.partial(grad_rows_end_kernel, turns=far, cuts=cuts),
        out_shape=(shape(rows, width), shape(width, rows)),
        in_specs=[whole(pltpu.SMEM)] * 2 + [whole()] * 2 + [weight],
        out_specs=(whole(), whole()),
        scratch_shapes=held(far),
        compiler_params=params(),
        name="grad_rows_end",
    )(at, suffix_length, first, grads[cuts // 2], out_weight)

    gathered, home_map = lax.optimization_barrier((gathered, home_map))
    keys = prefix_keys.shape[0] * per_prompt + rows
    attended, d_queries, d_suffix_keys, d_suffix_values, d_gathered = pl.pallas_call(
        functools.partial(attention_kernel, scale=HEAD_WIDTH**-0.5, together=4),
        out_shape=(
            shape(rows, width),
            shape(rows, width),
            shape(rows, HEAD_WIDTH),
            shape(rows, HEAD_WIDTH),
            shape(SERVERS, span, HEAD_WIDTH),
        ),
        in_specs=[whole(pltpu.SMEM)] + [whole()] * 6,
        out_specs=(whole(),) * 5,
        scratch_shapes=[
            pltpu.VMEM((keys, HEAD_WIDTH), BF16),
            pltpu.VMEM((keys, HEAD_WIDTH), BF16),
            pltpu.VMEM((keys, HEAD_WIDTH), F32),
            pltpu.VMEM((keys, HEAD_WIDTH), F32),
        ],
        compiler_params=params(),
        name="attention",
    )(suffix_length, queries, suffix_keys, suffix_values, gathered, d_rows, d_cols)

    def project(turns, own):
        return pl.pallas_call(
            functools.partial(project_kernel, turns=turns, cuts=cuts),
            out_shape=[shape(rows, features, dtype=F32 if d == own else BF16) for d in turns],
            in_specs=[whole(pltpu.SMEM), whole(), weight],
            out_specs=[whole()] * len(turns),
            scratch_shapes=held(turns),
            compiler_params=params(),
            name="project",
        )(at, attended, out_weight)

    terms_near = project(one_hop, 0)
    terms_far = project((cuts // 2, 0), 0)
    arrived = [turn(term, d) for d, term in zip(one_hop, terms_near)]
    projected = terms_far[1] + sum(x.astype(F32) for x in arrived)
    projected = projected + turn(terms_far[0], cuts // 2).astype(F32)

    terms, _ = lax.optimization_barrier((swap(d_gathered), (arrived, terms_far)))
    sums = pl.pallas_call(
        functools.partial(combine_kernel, turns=turns),
        out_shape=shape(homes * served, HEAD_WIDTH),
        in_specs=[whole(), whole(), whole()],
        out_specs=whole(),
        compiler_params=params(),
        name="combine",
    )(home_map, terms, swap_pairs(2 * prefix_rows, served // 2))
    back = lax.all_to_all(
        sums.reshape(homes, served, HEAD_WIDTH), "seq", 0, 0, tiled=True
    ).reshape(turns, 2 * prefix_rows, HEAD_WIDTH)
    d_prefix_keys, d_prefix_values = pl.pallas_call(
        home_sum_kernel,
        out_shape=(shape(prefix_rows, HEAD_WIDTH),) * 2,
        in_specs=[whole()],
        out_specs=(whole(), whole()),
        compiler_params=params(),
        name="home_sum",
    )(back)
    return (
        projected.astype(BF16),
        d_queries,
        d_suffix_keys,
        d_suffix_values,
        d_prefix_keys,
        d_prefix_values,
    )


def solution(mesh):
    split = P("seq", "tensor")
    in_specs = (split,) * 5 + (P("seq"),) * 3 + (P("tensor", None), split)
    return jax.shard_map(
        shards, mesh=mesh, in_specs=in_specs, out_specs=(split,) * 6, check_vma=False
    )
```

```python
import functools

import jax
import jax.numpy as jnp
import numpy as np
from jax import lax
from jax.experimental import pallas as pl
from jax.experimental.pallas import tpu as pltpu
from jax.sharding import PartitionSpec as P

HEAD_WIDTH = 128
PROMPTS = 8
SERVERS = 16
F32 = jnp.float32
BF16 = jnp.bfloat16
NT = (((1,), (1,)), ((), ()))


def dot(a, b):
    return jnp.dot(a, b, preferred_element_type=F32)


def dot_nt(a, b):
    return lax.dot_general(a, b, NT, preferred_element_type=F32)


def iota(shape, dim):
    return lax.broadcasted_iota(jnp.int32, shape, dim)


def one_hot(left, right):
    return (left == right).astype(BF16)


def fiota(shape, dim):
    return iota(shape, dim).astype(F32)


def pack_kernel(
    block_ref, rollout_ref, keys_hbm, values_hbm, sent_ref, keys_ref, values_ref, sems, *, rows, turns
):
    copies = [
        pltpu.make_async_copy(keys_hbm, keys_ref, sems.at[0]),
        pltpu.make_async_copy(values_hbm, values_ref, sems.at[1]),
    ]
    for copy in copies:
        copy.start()
    total, tall = keys_ref.shape[0], sent_ref.shape[0] // turns
    group = rows + 2
    row, col = iota((tall, total), 0), iota((tall, total), 1)
    place = row % group
    source = jnp.where(place < rows, (row // group) * rows + place, -1)
    take_keys, take_values = one_hot(source, col), one_hot(source - total, col)
    for copy in copies:
        copy.wait()
    packed = dot(take_keys, keys_ref[...])
    packed = packed + dot(take_values, values_ref[...])
    row, lane = iota(packed.shape, 0), iota(packed.shape, 1)
    names = jnp.where(lane == 0, block_ref[0], jnp.where(lane == 1, rollout_ref[0], 0))
    packed = jnp.where(row % group >= rows, names.astype(F32), packed).astype(BF16)
    for g in range(turns):
        sent_ref[g * tall : (g + 1) * tall, :] = packed


def swap_pairs(tall, outer):
    rows = np.arange(tall).reshape(outer, -1, 2).swapaxes(0, 1).reshape(tall)
    return jnp.asarray(np.eye(tall)[rows], BF16)


def name_rows(blocks, group):
    take = np.zeros((blocks, blocks, group))
    take[np.arange(blocks), np.arange(blocks), group - 2] = 1
    return jnp.asarray(take.reshape(blocks, blocks * group), BF16)


def block_codes(meta, *, per_prompt):
    blocks = meta.shape[0]
    first_lane = one_hot(iota((8, 128), 1), 0)
    prompt_row = dot_nt(first_lane, meta)[0:1]
    same = meta[:, 0:1].astype(F32) == prompt_row
    before = iota((blocks, blocks), 0) < iota((blocks, blocks), 1)
    rank = jnp.sum(jnp.where(jnp.logical_and(same, before), 1.0, 0.0), axis=0, keepdims=True)
    return prompt_row * per_prompt + rank


def own_rollouts(meta, own, *, servers, span):
    wants, blocks = servers * span, meta.shape[0]
    take = one_hot(iota((wants, blocks), 0) // span + own * servers, iota((wants, blocks), 1))
    return dot(take, meta)[:, 1:2]


def select_kernel(
    own_ref,
    pieces_ref,
    swap_ref,
    take_ref,
    picked_ref,
    meta_ref,
    *,
    per_prompt,
    servers,
    rows,
    turns,
):
    tall, blocks = servers * (rows + 2), servers * turns
    each, span = 2 * servers, 2 * per_prompt
    wants = span * servers
    meta = dot(take_ref[...], pieces_ref[...]).astype(BF16)
    meta_ref[...] = meta
    swap = swap_ref[...]
    pieces = [
        dot(swap, pieces_ref[g * tall : (g + 1) * tall]).astype(BF16) for g in range(turns)
    ]
    code = jnp.broadcast_to(block_codes(meta, per_prompt=per_prompt), (8, blocks))
    spread = one_hot(iota((blocks, 2 * blocks), 1) // 2, iota((blocks, 2 * blocks), 0))
    have = dot(code.astype(BF16), spread)[0:1] * 2
    have = have + (iota((1, 2 * blocks), 1) % 2).astype(F32)
    want = own_rollouts(meta, own_ref[0], servers=servers, span=span) * span
    want = want + (iota((wants, 1), 0) % span).astype(F32)
    choose = one_hot(want, have)
    for p in range(rows // 2):
        from_all = jnp.concatenate([part[p * each : (p + 1) * each] for part in pieces])
        picked = dot(choose, from_all).astype(BF16)
        picked_ref[:, p * span : (p + 1) * span, :] = picked.reshape(servers, span, HEAD_WIDTH)


def map_kernel(own_ref, meta_ref, map_ref, *, per_prompt, servers):
    meta = meta_ref[...]
    blocks = meta.shape[0]
    tall, wants = map_ref.shape
    span = 2 * per_prompt
    code_row = block_codes(meta, per_prompt=per_prompt)
    mine = iota((tall, blocks), 0) // 2 == iota((tall, blocks), 1)
    have = jnp.sum(jnp.where(mine, code_row, 0.0), axis=1, keepdims=True) * 2
    have = have + (iota((tall, 1), 0) % 2).astype(F32)
    rollout = own_rollouts(meta, own_ref[0], servers=servers, span=1)
    spread = iota((servers, wants), 1) // span == iota((servers, wants), 0)
    want = jnp.sum(jnp.where(spread, rollout, 0.0), axis=0, keepdims=True) * span
    want = want + (iota((1, wants), 1) % span).astype(F32)
    map_ref[...] = one_hot(have, want)


def combine_kernel(map_ref, terms_ref, swap_ref, out_ref, *, turns):
    servers, tall, _ = terms_ref.shape
    wants = map_ref.shape[1]
    span, each = wants // servers, map_ref.shape[0] // turns
    sums = []
    for p in range(tall // span):
        terms = terms_ref[:, p * span : (p + 1) * span, :].reshape(wants, HEAD_WIDTH)
        sums.append(dot(map_ref[...], terms).astype(BF16))
    rows = each * len(sums)
    swap = swap_ref[...]
    for g in range(turns):
        part = jnp.concatenate([s[g * each : (g + 1) * each] for s in sums])
        out_ref[g * rows : (g + 1) * rows, :] = dot(swap, part).astype(BF16)


def home_sum_kernel(terms_ref, keys_ref, values_ref):
    total = jnp.sum(terms_ref[...].astype(F32), axis=0)
    half = keys_ref.shape[0]
    keys_ref[...] = total[:half].astype(BF16)
    values_ref[...] = total[half:].astype(BF16)


def fetch(at_ref, w_ref, held, sems, turns, cuts):
    width = held.shape[2]
    copies = []
    for i, d in enumerate(turns):
        start = pl.multiple_of(lax.rem(at_ref[0] + d, cuts) * width, width)
        copies.append(
            pltpu.make_async_copy(w_ref.at[:, pl.ds(start, width)], held.at[i], sems.at[i])
        )
        copies[i].start()
    return copies


def grad_rows_kernel(at_ref, *refs, turns, cuts, after):
    refs, (held, sems) = refs[:-2], refs[-2:]
    count = len(refs) - 2 - len(after)
    in_refs, w_ref, total_ref = refs[:count], refs[count], refs[count + 1]
    copies = fetch(at_ref, w_ref, held, sems, turns + after, cuts)
    total = in_refs[-1][...] if count > len(turns) else None
    for i in range(len(turns)):
        copies[i].wait()
        term = dot_nt(held[i], in_refs[i][...])
        total = term if total is None else total + term
    total_ref[...] = total
    for i, ref in enumerate(refs[count + 2 :]):
        copies[len(turns) + i].wait()
        ref[...] = held[len(turns) + i]


def grad_rows_end_kernel(len_ref, first_ref, g_ref, w_ref, rows_ref, cols_ref):
    total = first_ref[...] + dot_nt(w_ref[...], g_ref[...])
    live = iota(total.shape, 1) < len_ref[0]
    total = jnp.where(live, total, 0.0)
    cols_ref[...] = total.astype(BF16)
    for h in range(total.shape[0] // HEAD_WIDTH):
        part = slice(h * HEAD_WIDTH, (h + 1) * HEAD_WIDTH)
        rows_ref[:, part] = total[part].T.astype(BF16)


def project_kernel(at_ref, a_ref, w_ref, *refs, turns, cuts):
    *out_refs, held, sems = refs
    for i, copy in enumerate(fetch(at_ref, w_ref, held, sems, turns, cuts)):
        copy.wait()
        out_refs[i][...] = dot(a_ref[...], held[i]).astype(out_refs[i].dtype)


def attention_kernel(
    len_ref,
    q_ref,
    ks_ref,
    vs_ref,
    g_ref,
    da_ref,
    dat_ref,
    att_ref,
    dq_ref,
    dks_ref,
    dvs_ref,
    dg_ref,
    k_all,
    v_all,
    dk_acc,
    dv_acc,
    *,
    scale,
    together,
):
    n = len_ref[0]
    half = g_ref.shape[0] // 2
    prefix = half * g_ref.shape[1]
    suffix = ks_ref.shape[0]
    k_all[:prefix, :] = g_ref[:half].reshape(prefix, HEAD_WIDTH)
    v_all[:prefix, :] = g_ref[half:].reshape(prefix, HEAD_WIDTH)
    k_all[prefix:, :] = ks_ref[...]
    v_all[prefix:, :] = vs_ref[...]
    k_t = k_all[...].T
    v_t = v_all[...].T
    lanes = together * suffix
    key_at = iota((suffix, lanes), 0)
    slot_at = iota((suffix, lanes), 1) % suffix
    hidden = jnp.logical_or(key_at > slot_at, key_at >= n)
    live = iota((1, lanes), 1) % suffix < n
    to_log2 = scale * 1.4426950408889634
    steps = q_ref.shape[1] // (together * HEAD_WIDTH)

    def heads(step):
        first = step * together
        return [slice((first + i) * HEAD_WIDTH, (first + i + 1) * HEAD_WIDTH) for i in range(together)]

    def rows_of(ref, step):
        return jnp.concatenate([ref[:, h] for h in heads(step)], axis=0)

    def put_rows(ref, step, x):
        for i, h in enumerate(heads(step)):
            ref[:, h] = x[:, i * suffix : (i + 1) * suffix].T.astype(BF16)

    def scores(step):
        s = dot_nt(k_all[...], rows_of(q_ref, step))
        return s[:prefix], jnp.where(hidden, -jnp.inf, s[prefix:])

    def softmax(s):
        peak = jnp.maximum(*[jnp.max(part, axis=0, keepdims=True) for part in s])
        parts = [jnp.exp2((part - peak) * to_log2) for part in s]
        total = sum(jnp.sum(part, axis=0, keepdims=True) for part in parts)
        w = jnp.concatenate(parts, axis=0)
        return w, w.astype(BF16), 1.0 / total

    ready = softmax(scores(0))
    for step in range(steps):
        last = step + 1 == steps
        if not last:
            coming = scores(step + 1)
        w, w_rounded, inverse = ready
        out_t = dot(v_t, w_rounded) * inverse
        out_t = jnp.where(live, out_t, 0.0).astype(BF16).astype(F32)
        put_rows(att_ref, step, out_t)
        dat = jnp.concatenate([dat_ref[h, :] for h in heads(step)], axis=1)
        dots = jnp.sum(out_t * dat.astype(F32), axis=0, keepdims=True)
        if not last:
            ready = softmax(coming)
        probs = w * inverse
        dv = dot(probs.astype(BF16), rows_of(da_ref, step))
        ds = (probs * (dot(v_all[...], dat) - dots)).astype(BF16)
        put_rows(dq_ref, step, dot(k_t, ds) * scale)
        dk = dot(ds, rows_of(q_ref, step))
        if step == 0:
            dk_acc[...] = dk
            dv_acc[...] = dv
        else:
            dk_acc[...] += dk
            dv_acc[...] += dv
    dg_ref[:half] = (dk_acc[:prefix] * scale).astype(BF16).reshape(half, -1, HEAD_WIDTH)
    dg_ref[half:] = dv_acc[:prefix].astype(BF16).reshape(half, -1, HEAD_WIDTH)
    dks_ref[...] = (dk_acc[prefix:] * scale).astype(BF16)
    dvs_ref[...] = dv_acc[prefix:].astype(BF16)


def in_hbm(x):
    return pltpu.with_memory_space_constraint(x, pltpu.HBM)


def whole(memory=pltpu.VMEM):
    return pl.BlockSpec(memory_space=memory)


def params(mib=24):
    return pltpu.CompilerParams(vmem_limit_bytes=mib * 1024 * 1024)


def shape(*dims, dtype=BF16):
    return jax.ShapeDtypeStruct(dims, dtype)


def shards(
    queries,
    suffix_keys,
    suffix_values,
    prefix_keys,
    prefix_values,
    block_prompt,
    rollout_prompt,
    suffix_length,
    out_weight,
    out_grad,
):
    homes = lax.axis_size("seq")
    cuts = lax.axis_size("tensor")
    rows, width = queries.shape
    features = out_grad.shape[1]
    per_prompt = homes // PROMPTS
    prefix_rows = prefix_keys.shape[0]
    served = 2 * prefix_rows // SERVERS
    tall = SERVERS * (served + 2)
    span = per_prompt * served
    groups = [[g + i for i in range(SERVERS)] for g in range(0, homes, SERVERS)]
    at = lax.axis_index("tensor").astype(jnp.int32).reshape(1)

    def swap(x):
        return lax.all_to_all(x, "seq", 0, 0, tiled=True, axis_index_groups=groups)

    turn = lambda x, d: lax.ppermute(x, "tensor", [(i, (i + d) % cuts) for i in range(cuts)])
    grads = [out_grad] + [turn(out_grad, cuts - d) for d in range(1, cuts)]
    weight = whole(pltpu.HBM)
    out_weight = in_hbm(out_weight)

    def held(turns):
        return [
            pltpu.VMEM((len(turns), width, features), BF16),
            pltpu.SemaphoreType.DMA((len(turns),)),
        ]

    def grad_rows(turns, before, after):
        return pl.pallas_call(
            functools.partial(grad_rows_kernel, turns=turns, cuts=cuts, after=after),
            out_shape=[shape(width, rows, dtype=F32)] + [shape(width, features)] * len(after),
            in_specs=[whole(pltpu.SMEM)] + [whole()] * (len(turns) + len(before)) + [weight],
            out_specs=[whole()] * (1 + len(after)),
            scratch_shapes=held(turns + after),
            compiler_params=params(),
            name="grad_rows",
        )(at, *[grads[d] for d in turns], *before, out_weight)

    one_hop = tuple(d for d in range(1, cuts) if d != cuts // 2)
    far = (cuts // 2,)
    (own_terms,) = grad_rows((0,), (), ())

    turns = homes // SERVERS
    own = (lax.axis_index("seq") // SERVERS).astype(jnp.int32).reshape(1)
    sent = pl.pallas_call(
        functools.partial(pack_kernel, rows=served, turns=turns),
        out_shape=shape(turns * tall, HEAD_WIDTH),
        in_specs=[whole(pltpu.SMEM)] * 2 + [whole(pltpu.HBM)] * 2,
        out_specs=whole(),
        scratch_shapes=[
            pltpu.VMEM(prefix_keys.shape, BF16),
            pltpu.VMEM(prefix_keys.shape, BF16),
            pltpu.SemaphoreType.DMA((2,)),
        ],
        compiler_params=params(),
        name="pack",
    )(block_prompt, rollout_prompt, in_hbm(prefix_keys), in_hbm(prefix_values))
    pieces = lax.all_to_all(
        sent.reshape(homes, served // 2 + 1, 2, HEAD_WIDTH), "seq", 0, 0, tiled=True
    ).reshape(turns * tall, HEAD_WIDTH)
    pieces, own_terms, grads[1], grads[-1] = lax.optimization_barrier(
        (pieces, own_terms, grads[1], grads[-1])
    )
    first, far_weight = grad_rows(one_hop, [own_terms], far)
    picked, meta = pl.pallas_call(
        functools.partial(
            select_kernel, per_prompt=per_prompt, servers=SERVERS, rows=served, turns=turns
        ),
        out_shape=(shape(SERVERS, span, HEAD_WIDTH), shape(homes, 128)),
        in_specs=[whole(pltpu.SMEM)] + [whole()] * 3,
        out_specs=(whole(), whole()),
        compiler_params=params(),
        name="select",
    )(own, pieces, swap_pairs(tall, SERVERS), name_rows(homes, served + 2))
    gathered = swap(picked)
    home_map = pl.pallas_call(
        functools.partial(map_kernel, per_prompt=per_prompt, servers=SERVERS),
        out_shape=shape(2 * homes, 2 * per_prompt * SERVERS),
        in_specs=[whole(pltpu.SMEM), whole()],
        out_specs=whole(),
        compiler_params=params(),
        name="home_map",
    )(own, meta)

    d_rows, d_cols = pl.pallas_call(
        grad_rows_end_kernel,
        out_shape=(shape(rows, width), shape(width, rows)),
        in_specs=[whole(pltpu.SMEM)] + [whole()] * 3,
        out_specs=(whole(), whole()),
        compiler_params=params(),
        name="grad_rows_end",
    )(suffix_length, first, grads[cuts // 2], far_weight)

    gathered, home_map = lax.optimization_barrier((gathered, home_map))
    keys = prefix_keys.shape[0] * per_prompt + rows
    attended, d_queries, d_suffix_keys, d_suffix_values, d_gathered = pl.pallas_call(
        functools.partial(attention_kernel, scale=HEAD_WIDTH**-0.5, together=4),
        out_shape=(
            shape(rows, width),
            shape(rows, width),
            shape(rows, HEAD_WIDTH),
            shape(rows, HEAD_WIDTH),
            shape(SERVERS, span, HEAD_WIDTH),
        ),
        in_specs=[whole(pltpu.SMEM)] + [whole()] * 6,
        out_specs=(whole(),) * 5,
        scratch_shapes=[
            pltpu.VMEM((keys, HEAD_WIDTH), BF16),
            pltpu.VMEM((keys, HEAD_WIDTH), BF16),
            pltpu.VMEM((keys, HEAD_WIDTH), F32),
            pltpu.VMEM((keys, HEAD_WIDTH), F32),
        ],
        compiler_params=params(),
        name="attention",
    )(suffix_length, queries, suffix_keys, suffix_values, gathered, d_rows, d_cols)

    def project(turns, own):
        return pl.pallas_call(
            functools.partial(project_kernel, turns=turns, cuts=cuts),
            out_shape=[shape(rows, features, dtype=F32 if d == own else BF16) for d in turns],
            in_specs=[whole(pltpu.SMEM), whole(), weight],
            out_specs=[whole()] * len(turns),
            scratch_shapes=held(turns),
            compiler_params=params(),
            name="project",
        )(at, attended, out_weight)

    terms_near = project(one_hop, 0)
    terms_far = project((cuts // 2, 0), 0)
    arrived = [turn(term, d) for d, term in zip(one_hop, terms_near)]
    projected = terms_far[1] + sum(x.astype(F32) for x in arrived)
    projected = projected + turn(terms_far[0], cuts // 2).astype(F32)

    terms, _ = lax.optimization_barrier((swap(d_gathered), (arrived, terms_far)))
    sums = pl.pallas_call(
        functools.partial(combine_kernel, turns=turns),
        out_shape=shape(homes * served, HEAD_WIDTH),
        in_specs=[whole(), whole(), whole()],
        out_specs=whole(),
        compiler_params=params(),
        name="combine",
    )(home_map, terms, swap_pairs(2 * prefix_rows, served // 2))
    back = lax.all_to_all(
        sums.reshape(homes, served, HEAD_WIDTH), "seq", 0, 0, tiled=True
    ).reshape(turns, 2 * prefix_rows, HEAD_WIDTH)
    d_prefix_keys, d_prefix_values = pl.pallas_call(
        home_sum_kernel,
        out_shape=(shape(prefix_rows, HEAD_WIDTH),) * 2,
        in_specs=[whole()],
        out_specs=(whole(), whole()),
        compiler_params=params(),
        name="home_sum",
    )(back)
    return (
        projected.astype(BF16),
        d_queries,
        d_suffix_keys,
        d_suffix_values,
        d_prefix_keys,
        d_prefix_values,
    )


def solution(mesh):
    split = P("seq", "tensor")
    in_specs = (split,) * 5 + (P("seq"),) * 3 + (P("tensor", None), split)
    return jax.shard_map(
        shards, mesh=mesh, in_specs=in_specs, out_specs=(split,) * 6, check_vma=False
    )
```

```python
import functools

import jax
import jax.numpy as jnp
import numpy as np
from jax import lax
from jax.experimental import pallas as pl
from jax.experimental.pallas import tpu as pltpu
from jax.sharding import PartitionSpec as P

HEAD_WIDTH = 128
PROMPTS = 8
SERVERS = 16
F32 = jnp.float32
BF16 = jnp.bfloat16
NT = (((1,), (1,)), ((), ()))


def dot(a, b):
    return jnp.dot(a, b, preferred_element_type=F32)


def dot_nt(a, b):
    return lax.dot_general(a, b, NT, preferred_element_type=F32)


def iota(shape, dim):
    return lax.broadcasted_iota(jnp.int32, shape, dim)


def one_hot(left, right):
    return (left == right).astype(BF16)


def fiota(shape, dim):
    return iota(shape, dim).astype(F32)


def pack_kernel(
    block_ref, rollout_ref, keys_hbm, values_hbm, sent_ref, keys_ref, values_ref, sems, *, rows, turns
):
    copies = [
        pltpu.make_async_copy(keys_hbm, keys_ref, sems.at[0]),
        pltpu.make_async_copy(values_hbm, values_ref, sems.at[1]),
    ]
    for copy in copies:
        copy.start()
    total, tall = keys_ref.shape[0], sent_ref.shape[0] // turns
    group = rows + 2
    row, col = iota((tall, total), 0), iota((tall, total), 1)
    place = row % group
    source = jnp.where(place < rows, (row // group) * rows + place, -1)
    take_keys, take_values = one_hot(source, col), one_hot(source - total, col)
    for copy in copies:
        copy.wait()
    packed = dot(take_keys, keys_ref[...])
    packed = packed + dot(take_values, values_ref[...])
    row, lane = iota(packed.shape, 0), iota(packed.shape, 1)
    names = jnp.where(lane == 0, block_ref[0], jnp.where(lane == 1, rollout_ref[0], 0))
    packed = jnp.where(row % group >= rows, names.astype(F32), packed).astype(BF16)
    for g in range(turns):
        sent_ref[g * tall : (g + 1) * tall, :] = packed


def swap_pairs(tall, outer):
    rows = np.arange(tall).reshape(outer, -1, 2).swapaxes(0, 1).reshape(tall)
    return jnp.asarray(np.eye(tall)[rows], BF16)


def name_rows(blocks, group):
    take = np.zeros((blocks, blocks, group))
    take[np.arange(blocks), np.arange(blocks), group - 2] = 1
    return jnp.asarray(take.reshape(blocks, blocks * group), BF16)


def block_codes(meta, *, per_prompt):
    blocks = meta.shape[0]
    first_lane = one_hot(iota((8, 128), 1), 0)
    prompt_row = dot_nt(first_lane, meta)[0:1]
    same = meta[:, 0:1].astype(F32) == prompt_row
    before = iota((blocks, blocks), 0) < iota((blocks, blocks), 1)
    rank = jnp.sum(jnp.where(jnp.logical_and(same, before), 1.0, 0.0), axis=0, keepdims=True)
    return prompt_row * per_prompt + rank


def own_rollouts(meta, own, *, servers, span):
    wants, blocks = servers * span, meta.shape[0]
    take = one_hot(iota((wants, blocks), 0) // span + own * servers, iota((wants, blocks), 1))
    return dot(take, meta)[:, 1:2]


def select_kernel(
    own_ref,
    pieces_ref,
    swap_ref,
    take_ref,
    picked_ref,
    meta_ref,
    *,
    per_prompt,
    servers,
    rows,
    turns,
):
    tall, blocks = servers * (rows + 2), servers * turns
    each, span = 2 * servers, 2 * per_prompt
    wants = span * servers
    meta = dot(take_ref[...], pieces_ref[...]).astype(BF16)
    meta_ref[...] = meta
    swap = swap_ref[...]
    pieces = [
        dot(swap, pieces_ref[g * tall : (g + 1) * tall]).astype(BF16) for g in range(turns)
    ]
    code = jnp.broadcast_to(block_codes(meta, per_prompt=per_prompt), (8, blocks))
    spread = one_hot(iota((blocks, 2 * blocks), 1) // 2, iota((blocks, 2 * blocks), 0))
    have = dot(code.astype(BF16), spread)[0:1] * 2
    have = have + (iota((1, 2 * blocks), 1) % 2).astype(F32)
    want = own_rollouts(meta, own_ref[0], servers=servers, span=span) * span
    want = want + (iota((wants, 1), 0) % span).astype(F32)
    choose = one_hot(want, have)
    for p in range(rows // 2):
        from_all = jnp.concatenate([part[p * each : (p + 1) * each] for part in pieces])
        picked = dot(choose, from_all).astype(BF16)
        picked_ref[:, p * span : (p + 1) * span, :] = picked.reshape(servers, span, HEAD_WIDTH)


def map_kernel(own_ref, meta_ref, map_ref, *, per_prompt, servers):
    meta = meta_ref[...]
    blocks = meta.shape[0]
    tall, wants = map_ref.shape
    span = 2 * per_prompt
    code_row = block_codes(meta, per_prompt=per_prompt)
    mine = iota((tall, blocks), 0) // 2 == iota((tall, blocks), 1)
    have = jnp.sum(jnp.where(mine, code_row, 0.0), axis=1, keepdims=True) * 2
    have = have + (iota((tall, 1), 0) % 2).astype(F32)
    rollout = own_rollouts(meta, own_ref[0], servers=servers, span=1)
    spread = iota((servers, wants), 1) // span == iota((servers, wants), 0)
    want = jnp.sum(jnp.where(spread, rollout, 0.0), axis=0, keepdims=True) * span
    want = want + (iota((1, wants), 1) % span).astype(F32)
    map_ref[...] = one_hot(have, want)


def combine_kernel(map_ref, terms_ref, swap_ref, out_ref, *, turns):
    servers, tall, _ = terms_ref.shape
    wants = map_ref.shape[1]
    span, each = wants // servers, map_ref.shape[0] // turns
    sums = []
    for p in range(tall // span):
        terms = terms_ref[:, p * span : (p + 1) * span, :].reshape(wants, HEAD_WIDTH)
        sums.append(dot(map_ref[...], terms).astype(BF16))
    rows = each * len(sums)
    swap = swap_ref[...]
    for g in range(turns):
        part = jnp.concatenate([s[g * each : (g + 1) * each] for s in sums])
        out_ref[g * rows : (g + 1) * rows, :] = dot(swap, part).astype(BF16)


def home_sum_kernel(terms_ref, keys_ref, values_ref):
    total = jnp.sum(terms_ref[...].astype(F32), axis=0)
    half = keys_ref.shape[0]
    keys_ref[...] = total[:half].astype(BF16)
    values_ref[...] = total[half:].astype(BF16)


def fetch(at_ref, w_ref, held, sems, turns, cuts):
    width = held.shape[2]
    copies = []
    for i, d in enumerate(turns):
        start = pl.multiple_of(lax.rem(at_ref[0] + d, cuts) * width, width)
        copies.append(
            pltpu.make_async_copy(w_ref.at[:, pl.ds(start, width)], held.at[i], sems.at[i])
        )
        copies[i].start()
    return copies


def grad_rows_kernel(at_ref, *refs, turns, cuts, after):
    refs, (held, sems) = refs[:-2], refs[-2:]
    count = len(refs) - 2 - len(after)
    in_refs, w_ref, total_ref = refs[:count], refs[count], refs[count + 1]
    copies = fetch(at_ref, w_ref, held, sems, turns + after, cuts)
    total = in_refs[-1][...] if count > len(turns) else None
    for i in range(len(turns)):
        copies[i].wait()
        term = dot_nt(held[i], in_refs[i][...])
        total = term if total is None else total + term
    total_ref[...] = total
    for i, ref in enumerate(refs[count + 2 :]):
        copies[len(turns) + i].wait()
        ref[...] = held[len(turns) + i]


def grad_rows_end_kernel(len_ref, first_ref, g_ref, w_ref, rows_ref, cols_ref):
    total = first_ref[...] + dot_nt(w_ref[...], g_ref[...])
    live = iota(total.shape, 1) < len_ref[0]
    total = jnp.where(live, total, 0.0)
    cols_ref[...] = total.astype(BF16)
    for h in range(total.shape[0] // HEAD_WIDTH):
        part = slice(h * HEAD_WIDTH, (h + 1) * HEAD_WIDTH)
        rows_ref[:, part] = total[part].T.astype(BF16)


def project_kernel(at_ref, a_ref, w_ref, *refs, turns, cuts):
    *out_refs, held, sems = refs
    for i, copy in enumerate(fetch(at_ref, w_ref, held, sems, turns, cuts)):
        copy.wait()
        out_refs[i][...] = dot(a_ref[...], held[i]).astype(out_refs[i].dtype)


def attention_kernel(
    len_ref,
    q_ref,
    ks_ref,
    vs_ref,
    g_ref,
    da_ref,
    dat_ref,
    att_ref,
    dq_ref,
    dks_ref,
    dvs_ref,
    dg_ref,
    k_all,
    v_all,
    dk_acc,
    dv_acc,
    *,
    scale,
    together,
):
    n = len_ref[0]
    half = g_ref.shape[0] // 2
    prefix = half * g_ref.shape[1]
    suffix = ks_ref.shape[0]
    k_all[:prefix, :] = g_ref[:half].reshape(prefix, HEAD_WIDTH)
    v_all[:prefix, :] = g_ref[half:].reshape(prefix, HEAD_WIDTH)
    k_all[prefix:, :] = ks_ref[...]
    v_all[prefix:, :] = vs_ref[...]
    k_t = k_all[...].T
    v_t = v_all[...].T
    lanes = together * suffix
    key_at = iota((suffix, lanes), 0)
    slot_at = iota((suffix, lanes), 1) % suffix
    hidden = jnp.logical_or(key_at > slot_at, key_at >= n)
    live = iota((1, lanes), 1) % suffix < n
    to_log2 = scale * 1.4426950408889634
    steps = q_ref.shape[1] // (together * HEAD_WIDTH)

    def heads(step):
        first = step * together
        return [slice((first + i) * HEAD_WIDTH, (first + i + 1) * HEAD_WIDTH) for i in range(together)]

    def rows_of(ref, step):
        return jnp.concatenate([ref[:, h] for h in heads(step)], axis=0)

    def put_rows(ref, step, x):
        for i, h in enumerate(heads(step)):
            ref[:, h] = x[:, i * suffix : (i + 1) * suffix].T.astype(BF16)

    def scores(step):
        s = dot_nt(k_all[...], rows_of(q_ref, step))
        return s[:prefix], jnp.where(hidden, -jnp.inf, s[prefix:])

    def softmax(s):
        peak = jnp.maximum(*[jnp.max(part, axis=0, keepdims=True) for part in s])
        parts = [jnp.exp2((part - peak) * to_log2) for part in s]
        total = sum(jnp.sum(part, axis=0, keepdims=True) for part in parts)
        w = jnp.concatenate(parts, axis=0)
        return w, w.astype(BF16), 1.0 / total

    ready = softmax(scores(0))
    for step in range(steps):
        last = step + 1 == steps
        if not last:
            coming = scores(step + 1)
        w, w_rounded, inverse = ready
        out_t = dot(v_t, w_rounded) * inverse
        out_t = jnp.where(live, out_t, 0.0).astype(BF16).astype(F32)
        put_rows(att_ref, step, out_t)
        dat = jnp.concatenate([dat_ref[h, :] for h in heads(step)], axis=1)
        dots = jnp.sum(out_t * dat.astype(F32), axis=0, keepdims=True)
        if not last:
            ready = softmax(coming)
        probs = w * inverse
        dv = dot(probs.astype(BF16), rows_of(da_ref, step))
        ds = (probs * (dot(v_all[...], dat) - dots)).astype(BF16)
        put_rows(dq_ref, step, dot(k_t, ds) * scale)
        dk = dot(ds, rows_of(q_ref, step))
        if step == 0:
            dk_acc[...] = dk
            dv_acc[...] = dv
        else:
            dk_acc[...] += dk
            dv_acc[...] += dv
    dg_ref[:half] = (dk_acc[:prefix] * scale).astype(BF16).reshape(half, -1, HEAD_WIDTH)
    dg_ref[half:] = dv_acc[:prefix].astype(BF16).reshape(half, -1, HEAD_WIDTH)
    dks_ref[...] = (dk_acc[prefix:] * scale).astype(BF16)
    dvs_ref[...] = dv_acc[prefix:].astype(BF16)


def in_hbm(x):
    return pltpu.with_memory_space_constraint(x, pltpu.HBM)


def whole(memory=pltpu.VMEM):
    return pl.BlockSpec(memory_space=memory)


def params(mib=24):
    return pltpu.CompilerParams(vmem_limit_bytes=mib * 1024 * 1024)


def shape(*dims, dtype=BF16):
    return jax.ShapeDtypeStruct(dims, dtype)


def shards(
    queries,
    suffix_keys,
    suffix_values,
    prefix_keys,
    prefix_values,
    block_prompt,
    rollout_prompt,
    suffix_length,
    out_weight,
    out_grad,
):
    homes = lax.axis_size("seq")
    cuts = lax.axis_size("tensor")
    rows, width = queries.shape
    features = out_grad.shape[1]
    per_prompt = homes // PROMPTS
    prefix_rows = prefix_keys.shape[0]
    served = 2 * prefix_rows // SERVERS
    tall = SERVERS * (served + 2)
    span = per_prompt * served
    groups = [[g + i for i in range(SERVERS)] for g in range(0, homes, SERVERS)]
    at = lax.axis_index("tensor").astype(jnp.int32).reshape(1)

    def swap(x):
        return lax.all_to_all(x, "seq", 0, 0, tiled=True, axis_index_groups=groups)

    turn = lambda x, d: lax.ppermute(x, "tensor", [(i, (i + d) % cuts) for i in range(cuts)])
    grads = [turn(out_grad, cuts - d) for d in range(cuts - 1, 0, -1)]
    grads = [out_grad] + grads[::-1]
    weight = whole(pltpu.HBM)
    out_weight = in_hbm(out_weight)

    def held(turns):
        return [
            pltpu.VMEM((len(turns), width, features), BF16),
            pltpu.SemaphoreType.DMA((len(turns),)),
        ]

    def grad_rows(turns, before, after):
        return pl.pallas_call(
            functools.partial(grad_rows_kernel, turns=turns, cuts=cuts, after=after),
            out_shape=[shape(width, rows, dtype=F32)] + [shape(width, features)] * len(after),
            in_specs=[whole(pltpu.SMEM)] + [whole()] * (len(turns) + len(before)) + [weight],
            out_specs=[whole()] * (1 + len(after)),
            scratch_shapes=held(turns + after),
            compiler_params=params(),
            name="grad_rows",
        )(at, *[grads[d] for d in turns], *before, out_weight)

    one_hop = tuple(d for d in range(1, cuts) if d != cuts // 2)
    far = (cuts // 2,)
    (own_terms,) = grad_rows((0,), (), ())

    turns = homes // SERVERS
    own = (lax.axis_index("seq") // SERVERS).astype(jnp.int32).reshape(1)
    sent = pl.pallas_call(
        functools.partial(pack_kernel, rows=served, turns=turns),
        out_shape=shape(turns * tall, HEAD_WIDTH),
        in_specs=[whole(pltpu.SMEM)] * 2 + [whole(pltpu.HBM)] * 2,
        out_specs=whole(),
        scratch_shapes=[
            pltpu.VMEM(prefix_keys.shape, BF16),
            pltpu.VMEM(prefix_keys.shape, BF16),
            pltpu.SemaphoreType.DMA((2,)),
        ],
        compiler_params=params(),
        name="pack",
    )(block_prompt, rollout_prompt, in_hbm(prefix_keys), in_hbm(prefix_values))
    pieces = lax.all_to_all(
        sent.reshape(homes, served // 2 + 1, 2, HEAD_WIDTH), "seq", 0, 0, tiled=True
    ).reshape(turns * tall, HEAD_WIDTH)
    pieces, own_terms, grads[-1], grads[1] = lax.optimization_barrier(
        (pieces, own_terms, grads[-1], grads[1])
    )
    first, far_weight = grad_rows(one_hop, [own_terms], far)
    picked, meta = pl.pallas_call(
        functools.partial(
            select_kernel, per_prompt=per_prompt, servers=SERVERS, rows=served, turns=turns
        ),
        out_shape=(shape(SERVERS, span, HEAD_WIDTH), shape(homes, 128)),
        in_specs=[whole(pltpu.SMEM)] + [whole()] * 3,
        out_specs=(whole(), whole()),
        compiler_params=params(),
        name="select",
    )(own, pieces, swap_pairs(tall, SERVERS), name_rows(homes, served + 2))
    gathered = swap(picked)
    home_map = pl.pallas_call(
        functools.partial(map_kernel, per_prompt=per_prompt, servers=SERVERS),
        out_shape=shape(2 * homes, 2 * per_prompt * SERVERS),
        in_specs=[whole(pltpu.SMEM), whole()],
        out_specs=whole(),
        compiler_params=params(),
        name="home_map",
    )(own, meta)

    d_rows, d_cols = pl.pallas_call(
        grad_rows_end_kernel,
        out_shape=(shape(rows, width), shape(width, rows)),
        in_specs=[whole(pltpu.SMEM)] + [whole()] * 3,
        out_specs=(whole(), whole()),
        compiler_params=params(),
        name="grad_rows_end",
    )(suffix_length, first, grads[cuts // 2], far_weight)

    gathered, home_map = lax.optimization_barrier((gathered, home_map))
    keys = prefix_keys.shape[0] * per_prompt + rows
    attended, d_queries, d_suffix_keys, d_suffix_values, d_gathered = pl.pallas_call(
        functools.partial(attention_kernel, scale=HEAD_WIDTH**-0.5, together=4),
        out_shape=(
            shape(rows, width),
            shape(rows, width),
            shape(rows, HEAD_WIDTH),
            shape(rows, HEAD_WIDTH),
            shape(SERVERS, span, HEAD_WIDTH),
        ),
        in_specs=[whole(pltpu.SMEM)] + [whole()] * 6,
        out_specs=(whole(),) * 5,
        scratch_shapes=[
            pltpu.VMEM((keys, HEAD_WIDTH), BF16),
            pltpu.VMEM((keys, HEAD_WIDTH), BF16),
            pltpu.VMEM((keys, HEAD_WIDTH), F32),
            pltpu.VMEM((keys, HEAD_WIDTH), F32),
        ],
        compiler_params=params(),
        name="attention",
    )(suffix_length, queries, suffix_keys, suffix_values, gathered, d_rows, d_cols)

    def project(turns, own):
        return pl.pallas_call(
            functools.partial(project_kernel, turns=turns, cuts=cuts),
            out_shape=[shape(rows, features, dtype=F32 if d == own else BF16) for d in turns],
            in_specs=[whole(pltpu.SMEM), whole(), weight],
            out_specs=[whole()] * len(turns),
            scratch_shapes=held(turns),
            compiler_params=params(),
            name="project",
        )(at, attended, out_weight)

    terms_near = project(one_hop, 0)
    terms_far = project((cuts // 2, 0), 0)
    arrived = [turn(term, d) for d, term in zip(one_hop, terms_near)]
    projected = terms_far[1] + sum(x.astype(F32) for x in arrived)
    projected = projected + turn(terms_far[0], cuts // 2).astype(F32)

    terms, _ = lax.optimization_barrier((swap(d_gathered), (arrived, terms_far)))
    sums = pl.pallas_call(
        functools.partial(combine_kernel, turns=turns),
        out_shape=shape(homes * served, HEAD_WIDTH),
        in_specs=[whole(), whole(), whole()],
        out_specs=whole(),
        compiler_params=params(),
        name="combine",
    )(home_map, terms, swap_pairs(2 * prefix_rows, served // 2))
    back = lax.all_to_all(
        sums.reshape(homes, served, HEAD_WIDTH), "seq", 0, 0, tiled=True
    ).reshape(turns, 2 * prefix_rows, HEAD_WIDTH)
    d_prefix_keys, d_prefix_values = pl.pallas_call(
        home_sum_kernel,
        out_shape=(shape(prefix_rows, HEAD_WIDTH),) * 2,
        in_specs=[whole()],
        out_specs=(whole(), whole()),
        compiler_params=params(),
        name="home_sum",
    )(back)
    return (
        projected.astype(BF16),
        d_queries,
        d_suffix_keys,
        d_suffix_values,
        d_prefix_keys,
        d_prefix_values,
    )


def solution(mesh):
    split = P("seq", "tensor")
    in_specs = (split,) * 5 + (P("seq"),) * 3 + (P("tensor", None), split)
    return jax.shard_map(
        shards, mesh=mesh, in_specs=in_specs, out_specs=(split,) * 6, check_vma=False
    )
```
